512 devices in a mesh: field: 2 (over core), group: 8 (over y), row: 32 (over z, x).
Axes of the slice: x: 4, y: 8, z: 8, core: 2. Of those that a mesh axis runs over, the one named last changes fastest.
Arguments:
- anomalies: bfloat16 [2, 262144, 512], P('field', ('group', 'row')), may hold values from -6 to 6
- valid_rows: int32 [2, 256], P('field', ('group', 'row')), may hold values from 512 to 1024
- start_basis: float32 [512, 64], replicated, may hold values from -6 to 6
Outputs:
- patterns: float32 [2, 262144, 64], P('field', ('group', 'row'))
- strengths: float32 [64], replicated
The draws below stay inside these ranges and needn't reach their ends.
Inputs may be any that keep to these rules, and one draw needn't show every extreme that they name: `valid_rows`: the number of ocean points at the head of each shard; the rest of the shard is land and holds values that must be ignored.
All inputs are finite; a program needn't handle non-finite values.
Results may differ from the reference program's by a relative error of at most 0.0003.
Values sent between devices are 32-bit elements; how exact they have to be, the bound alone decides.
A program may use at most 64 MiB of HBM per device.

```python
import math
import jax
import jax.numpy as jnp
from jax import lax

MONTHS = 512
MODES = 64
ROWS_DEV = 1024
ITERS = 1
SHARDS = 256
ROWS = 262144


def one_field(field_key):
    pieces = jax.random.split(field_key, 2)
    white_noise = jax.random.normal(pieces[0], (ROWS, MONTHS + 2), jnp.float32)
    smoothed = (white_noise[:, 2:] + 0.6 * white_noise[:, 1:-1] + 0.4 * white_noise[:, :-2]) / math.sqrt(1.52)
    month_scale = jnp.exp(jax.random.uniform(pieces[1], (1, MONTHS), jnp.float32, math.log(0.5), math.log(2.0)))
    values = smoothed * month_scale
    return jnp.clip(values, -6.0, 6.0)


def draw_anomalies(key, part):
    field_keys = jax.random.split(jax.random.fold_in(key, 17), 2)
    return lax.map(one_field, field_keys).astype(jnp.bfloat16)


def set_ends(result, key, low, largest):
    longest = result.shape.index(max(result.shape))
    spots = []
    for shift in (0, 1):
        where = [jax.random.randint(jax.random.fold_in(key, axis), (), 0, length) for axis, length in enumerate(result.shape)]
        where[longest] = (where[longest] + shift) % result.shape[longest]
        spots.append(tuple(where))
    return result.at[spots[0]].set(low).at[spots[1]].set(largest)


def bell_draw(stream_key, shape, width, reach, kind=jnp.bfloat16):
    array = width * jax.random.normal(stream_key, shape, jnp.float32)
    return jnp.clip(array, min=-reach, max=reach).astype(kind)


def setup_inputs(seed: int = 0) -> dict:
    seeds = jax.random.split(jax.random.key(seed), 4)
    anomalies = draw_anomalies(jax.random.fold_in(seeds[3], 71), 0)
    valid_rows = set_ends(jax.random.randint(seeds[1], (2, SHARDS), ROWS_DEV // 2, ROWS_DEV + 1), jax.random.fold_in(seeds[1], 1), ROWS_DEV // 2, ROWS_DEV).astype(jnp.int32)
    start_basis = bell_draw(seeds[2], (MONTHS, MODES), 1.0, 6.0, jnp.float32)
    return {"anomalies": anomalies, "valid_rows": valid_rows, "start_basis": start_basis}


HIGH = lax.Precision.HIGHEST

def orthonormal(block):
    product = jnp.dot(block.T.astype(jnp.float32), block.astype(jnp.float32), precision=HIGH, preferred_element_type=jnp.float32)
    lower = jnp.linalg.cholesky(product)
    return lax.linalg.triangular_solve(lower, block, left_side=False, lower=True, transpose_a=True)

def masked_field(values, counts):
    index = jnp.arange(ROWS, dtype=jnp.int32)
    shard = index // ROWS_DEV
    place = index - shard * ROWS_DEV
    keep = place < counts[shard]
    return jnp.where(keep[:, None], values, jnp.zeros_like(values))

def upper_factor(masked, counts):
    gram = lax.dot_general(masked.astype(jnp.float32), masked.astype(jnp.float32), (((0,), (0,)), ((), ())), preferred_element_type=jnp.float32)
    total = jnp.sum(counts.astype(jnp.float32))
    return jnp.linalg.cholesky(gram / total).T

def project(masked, factor, basis):
    solved = lax.linalg.triangular_solve(factor, basis, left_side=True, lower=False)
    blocks = masked.reshape(SHARDS, ROWS_DEV, MONTHS)
    out = lax.map(lambda piece: jnp.dot(piece.astype(jnp.float32), solved.astype(jnp.float32), precision=HIGH, preferred_element_type=jnp.float32), blocks)
    return out.reshape(ROWS, MODES)

def reference(anomalies, valid_rows, start_basis):
    first = masked_field(anomalies[0], valid_rows[0])
    second = masked_field(anomalies[1], valid_rows[1])
    factor_one = upper_factor(first, valid_rows[0])
    factor_two = upper_factor(second, valid_rows[1])
    coupling = jnp.dot(factor_one.astype(jnp.float32), factor_two.T.astype(jnp.float32), precision=HIGH, preferred_element_type=jnp.float32)
    right = start_basis
    left = start_basis
    for step in range(ITERS):
        left = orthonormal(jnp.dot(coupling.astype(jnp.float32), right.astype(jnp.float32), precision=HIGH, preferred_element_type=jnp.float32))
        right = orthonormal(jnp.dot(coupling.T.astype(jnp.float32), left.astype(jnp.float32), precision=HIGH, preferred_element_type=jnp.float32))
    image = jnp.dot(coupling.astype(jnp.float32), right.astype(jnp.float32), precision=HIGH, preferred_element_type=jnp.float32)
    strengths = jnp.sum(left * image, axis=0)
    patterns = jnp.stack([project(first, factor_one, left), project(second, factor_two, right)])
    return (patterns, strengths)
```

```python
import functools

import jax
import jax.numpy as jnp
from jax import lax
from jax.experimental import pallas as pl
from jax.experimental.pallas import tpu as pltpu
from jax.sharding import PartitionSpec as P

F32, BF16 = jnp.float32, jnp.bfloat16
NN = (((1,), (0,)), ((), ()))
NT = (((1,), (1,)), ((), ()))
TN = (((0,), (0,)), ((), ()))
MESH = pl.DeviceIdType.MESH
NX, NY, NZ = 4, 8, 8
PIECE = 5
BLOCKS = [(i, j) for i in range(4) for j in range(i, 4)]
AT = {pair: at for at, pair in enumerate(BLOCKS)}


def split(x):
    hi = x.astype(BF16)
    return hi, (x - hi.astype(F32)).astype(BF16)


def mm(a, b, dims=NN):
    ah, al = split(a)
    bh, bl = split(b)
    dot = functools.partial(lax.dot_general, dimension_numbers=dims, preferred_element_type=F32)
    return dot(ah, bh) + (dot(ah, bl) + dot(al, bh))


def across(x, k):
    return jnp.broadcast_to(x[k : k + 1, :], (8, 128))


def along(x, k):
    return jnp.broadcast_to(x[:, k : k + 1], (8, 128))


def eliminate(panel, upper, weights, leaves):
    n = panel.shape[1] // 128
    rows = 8 * leaves
    sub = lax.broadcasted_iota(jnp.int32, (8, 128), 0)
    weights[...] = jnp.zeros_like(weights)
    pivots = []
    for leaf in range(leaves):
        at = 8 * leaf
        r = [panel[at : at + 8, 128 * j : 128 * j + 128] for j in range(n)]
        c = [along(r[0], at + k) for k in range(8)]
        scale = None
        for k in range(8):
            d = across(c[k], k)
            p = 1.0 / d
            root = lax.rsqrt(d)
            pivots.append(d[0:1] * root[0:1])
            scale = p if k == 0 else jnp.where(sub >= k, p, scale)
            m = jnp.where(sub == k, 0.0, c[k] * p)
            for j in range(n):
                row = across(r[j], k)
                upper[at + k : at + k + 1, 128 * j : 128 * j + 128] = (row * root)[0:1]
                r[j] = r[j] - m * row
            for j in range(k + 1, 8):
                c[j] = c[j] - m * across(c[j], k)
        if at + 8 == rows:
            break
        for j in range(n):
            weights[at : at + 8, 128 * j : 128 * j + 128] = r[j] * scale
        if leaf:
            weights[at - 8 : at, :] = jnp.zeros((8, 128 * n), F32)
        lhs = panel[at + 8 : rows, 0:128]
        panel[at + 8 : rows, :] -= mm(lhs, weights[...])
    return pivots


def masked_rows(values, ocean):
    place = lax.broadcasted_iota(jnp.int32, (values.shape[0], 1), 0)
    return jnp.where(place < ocean, values, jnp.zeros_like(values))


def gram_kernel(ocean_ref, values_ref, out_ref):
    ocean = ocean_ref[0, 0]
    masked = masked_rows(values_ref[...], ocean)
    row = lax.broadcasted_iota(jnp.int32, (128, 128), 0)
    col = lax.broadcasted_iota(jnp.int32, (128, 128), 1)
    corner = jnp.logical_and(row == 127, col == 0)
    for i in range(4):
        product = lax.dot_general(
            masked[:, 128 * i : 128 * i + 128], masked[:, 128 * i :], TN, preferred_element_type=F32
        )
        for j in range(i, 4):
            block = product[:, 128 * (j - i) : 128 * (j - i) + 128]
            if i == j == 0:
                block = jnp.where(corner, ocean.astype(F32), block)
            out_ref[AT[i, j]] = block


def reduce_kernel(g_ref, both_ref, from_x, sum_x, from_y, sum_y, from_z, sx, rx, sy, ry, sz, rz, say, ray, sax, rax, sc, rc):
    field = lax.axis_index("field")
    y = lax.axis_index("group")
    row = lax.axis_index("row")
    z, x = row // NX, row % NX

    def at_x(other):
        return (field, y, z * NX + other)

    def at_y(other):
        return (field, other, row)

    def at_z(other):
        return (field, y, other * NX + x)

    partner = (1 - field, y, row)
    xs = [(x + d) % NX for d in range(1, NX)]
    ys = [(y + d) % NY for d in range(1, NY)]
    zs = [(z + d) % NZ for d in range(1, NZ)]
    barrier = pltpu.get_barrier_semaphore()
    everyone = [at_x(o) for o in xs] + [at_y(o) for o in ys] + [at_z(o) for o in zs] + [partner]
    for device in everyone:
        pl.semaphore_signal(barrier, inc=1, device_id=device, device_id_type=MESH)
    pl.semaphore_wait(barrier, len(everyone))

    def send(src, dst, s, r, device):
        copy = pltpu.make_async_remote_copy(
            src_ref=src, dst_ref=dst, send_sem=s, recv_sem=r, device_id=device, device_id_type=MESH
        )
        copy.start()
        return copy

    started = []
    copies = [send(g_ref.at[xs[d]], from_x.at[d], sx.at[d], rx.at[d], at_x(xs[d])) for d in range(NX - 1)]
    for copy in copies:
        copy.wait_recv()
    started += copies
    sum_x[...] = g_ref[x] + from_x[0] + from_x[1] + from_x[2]

    copies = [send(sum_x.at[ys[d]], from_y.at[d], sy.at[d], ry.at[d], at_y(ys[d])) for d in range(NY - 1)]
    for copy in copies:
        copy.wait_recv()
    started += copies
    total = sum_x[y]
    for d in range(NY - 1):
        total = total + from_y[d]
    sum_y[...] = total

    copies = [send(sum_y, from_z.at[z], sz.at[d], rz.at[d], at_z(zs[d])) for d in range(NZ - 1)]
    from_z[z] = sum_y[...]
    for copy in copies:
        copy.wait_recv()
    started += copies
    total = from_z[0]
    for other in range(1, NZ):
        total = total + from_z[other]
    mine = both_ref.at[field]
    mine[x, y] = total

    copies = [send(mine.at[x, y], mine.at[x, y], say.at[d], ray.at[d], at_y(ys[d])) for d in range(NY - 1)]
    for copy in copies:
        copy.wait_recv()
    started += copies

    copies = [send(mine.at[x], mine.at[x], sax.at[d], rax.at[d], at_x(xs[d])) for d in range(NX - 1)]
    across_chip = [send(mine.at[x], mine.at[x], sc.at[0], rc.at[0], partner)]
    for d in range(NX - 1):
        copies[d].wait_recv()
        source = (x + NX - 1 - d) % NX
        across_chip.append(send(mine.at[source], mine.at[source], sc.at[d + 1], rc.at[d + 1], partner))
    started += copies
    for copy in across_chip:
        copy.wait_recv()
    for copy in started + across_chip:
        copy.wait_send()


def all_reduced(packed):
    sems = []
    for n in (NX - 1, NY - 1, NZ - 1, NY - 1, NX - 1, NX):
        sems += [pltpu.SemaphoreType.DMA((n,))] * 2
    vm = pl.BlockSpec(memory_space=pltpu.VMEM)
    return pl.pallas_call(
        reduce_kernel,
        out_shape=jax.ShapeDtypeStruct((2, NX, NY, PIECE, 8, 128), F32),
        in_specs=[vm],
        out_specs=vm,
        scratch_shapes=[
            pltpu.VMEM((NX - 1, NY, PIECE, 8, 128), F32),
            pltpu.VMEM((NY, PIECE, 8, 128), F32),
            pltpu.VMEM((NY - 1, PIECE, 8, 128), F32),
            pltpu.VMEM((PIECE, 8, 128), F32),
            pltpu.VMEM((NZ, PIECE, 8, 128), F32),
        ]
        + sems,
        compiler_params=pltpu.CompilerParams(
            collective_id=0, has_side_effects=True, vmem_limit_bytes=32 * 2**20
        ),
    )(packed)


def modes_kernel(ocean_ref, both_ref, st_ref, values_ref, out_ref, strengths_ref, a, u, w, e, eu, st0, fin, g0, *, field):
    row = lax.broadcasted_iota(jnp.int32, (128, 128), 0)
    col = lax.broadcasted_iota(jnp.int32, (128, 128), 1)
    corner = jnp.logical_and(row == 127, col == 0)
    which = ocean_ref[0, 1] if field is None else field

    def scaled(f, at, rate):
        block = both_ref[f, at]
        if at == 0:
            block = jnp.where(corner, block[0:1, 127:128], block)
        return block * rate

    rates = []
    for f in range(2):
        rates.append(1.0 / both_ref[f, 0][127:128, 0:1])
    for i, j in BLOCKS:
        a[128 * i : 128 * i + 128, 128 * j : 128 * j + 128] = scaled(1, AT[i, j], rates[1])
        g0[AT[i, j]] = scaled(0, AT[i, j], rates[0])
    for i in range(4):
        lo, n = 128 * i, 512 - 128 * i
        at = pl.ds(lo, 128)
        eliminate(a.at[at, lo:512], u.at[at, lo:512], w.at[:, 0:n], 16)
        for j in range(i + 1, 4):
            turned = u[lo : lo + 128, 128 * j : 128 * j + 128].T
            a[128 * j : 128 * j + 128, 128 * j : 512] -= mm(turned, u[lo : lo + 128, 128 * j : 512])

    for j in range(4):
        total = None
        for i in range(j + 1):
            block = u[128 * i : 128 * i + 128, 128 * j : 128 * j + 128]
            if i == j:
                block = jnp.where(row <= col, block, 0.0)
            term = mm(st_ref[:, 128 * i : 128 * i + 128], block)
            total = term if total is None else total + term
        e[:, 128 + 128 * j : 256 + 128 * j] = total

    def times_gram(left, block):
        done = []
        for j in range(4):
            total = None
            for i in range(4):
                piece = left[:, 128 * i : 128 * i + 128]
                term = mm(piece, block(i, j)) if i <= j else mm(piece, block(j, i), NT)
                total = term if total is None else total + term
            done.append(total)
        return jnp.concatenate(done, axis=1)

    xt = e[:, 128:640]
    zt = times_gram(xt, lambda i, j: g0[AT[i, j]])
    e[:, 640:1152] = zt
    e[:, 0:128] = jnp.concatenate([mm(xt, zt, NT), jnp.zeros((64, 64), F32)], axis=1)
    eliminate(e, eu, w, 8)
    fin[0] = eu[:, 128:640]
    yt = eu[:, 640:1152]
    ft = times_gram(yt, lambda i, j: scaled(1, AT[i, j], rates[1]))
    e[:, 0:128] = jnp.concatenate([mm(ft, yt, NT), jnp.zeros((64, 64), F32)], axis=1)
    e[:, 128:640] = yt
    pivots = eliminate(e.at[:, 0:640], eu.at[:, 0:640], w.at[:, 0:640], 8)
    fin[1] = eu[:, 128:640]
    lane = lax.broadcasted_iota(jnp.int32, (1, 128), 1)
    line = jnp.zeros((1, 128), F32)
    for k, pivot in enumerate(pivots):
        line = jnp.where(lane == k, pivot, line)
    strengths_ref[...] = line
    wh, wl = split(fin[which])
    masked = masked_rows(values_ref[...], ocean_ref[0, 0])
    dot = functools.partial(lax.dot_general, dimension_numbers=NT, preferred_element_type=F32)
    out_ref[...] = dot(masked, wh) + dot(masked, wl)


def modes(info, both, st, values, field=None):
    vm = pl.BlockSpec(memory_space=pltpu.VMEM)
    return pl.pallas_call(
        functools.partial(modes_kernel, field=field),
        out_shape=(jax.ShapeDtypeStruct((1024, 64), F32), jax.ShapeDtypeStruct((1, 128), F32)),
        in_specs=[pl.BlockSpec(memory_space=pltpu.SMEM), vm, vm, vm],
        out_specs=(vm, vm),
        scratch_shapes=[
            pltpu.VMEM((512, 512), F32),
            pltpu.VMEM((512, 512), F32),
            pltpu.VMEM((128, 1152), F32),
            pltpu.VMEM((64, 1152), F32),
            pltpu.VMEM((64, 1152), F32),
            pltpu.VMEM((64, 512), F32),
            pltpu.VMEM((2, 64, 512), F32),
            pltpu.VMEM((10, 128, 128), F32),
        ],
        compiler_params=pltpu.CompilerParams(vmem_limit_bytes=48 * 2**20),
    )(info, both.reshape(2, 10, 128, 128), st, values)


def gram(info, values):
    return pl.pallas_call(
        gram_kernel,
        out_shape=jax.ShapeDtypeStruct((10, 128, 128), F32),
        in_specs=[pl.BlockSpec(memory_space=pltpu.SMEM), pl.BlockSpec(memory_space=pltpu.VMEM)],
        out_specs=pl.BlockSpec(memory_space=pltpu.VMEM),
        compiler_params=pltpu.CompilerParams(vmem_limit_bytes=32 * 2**20),
    )(info, values)


def per_device(anomalies, valid_rows, start_basis):
    values = anomalies[0]
    which = lax.axis_index("field")
    info = jnp.concatenate([valid_rows, which.astype(jnp.int32).reshape(1, 1)], axis=1)
    packed = gram(info, values)
    both = all_reduced(packed.reshape(NX, NY, PIECE, 8, 128))
    patterns, strengths = modes(info, both, start_basis.T, values)
    return patterns[None], strengths[0, :64]


def solution(mesh):
    shards = ("group", "row")
    in_specs = (P("field", shards, None), P("field", shards), P())
    out_specs = (P("field", shards, None), P())
    return jax.shard_map(
        per_device, mesh=mesh, in_specs=in_specs, out_specs=out_specs, check_vma=False
    )
```

```python
import functools

import jax
import jax.numpy as jnp
from jax import lax
from jax.experimental import pallas as pl
from jax.experimental.pallas import tpu as pltpu
from jax.sharding import PartitionSpec as P

F32, BF16 = jnp.float32, jnp.bfloat16
NN = (((1,), (0,)), ((), ()))
NT = (((1,), (1,)), ((), ()))
TN = (((0,), (0,)), ((), ()))
MESH = pl.DeviceIdType.MESH
NX, NY, NZ = 4, 8, 8
PIECE = 5
TALL = 16
BLOCKS = [(i, j) for i in range(4) for j in range(i, 4)]
AT = {pair: at for at, pair in enumerate(BLOCKS)}


def split(x):
    hi = x.astype(BF16)
    return hi, (x - hi.astype(F32)).astype(BF16)


def mm(a, b, dims=NN):
    ah, al = split(a)
    bh, bl = split(b)
    dot = functools.partial(lax.dot_general, dimension_numbers=dims, preferred_element_type=F32)
    return dot(ah, bh) + (dot(ah, bl) + dot(al, bh))


def across(x, k):
    return jnp.broadcast_to(x[k : k + 1, :], (8, 128))


def along(x, k):
    return jnp.broadcast_to(x[:, k : k + 1], (8, 128))


def eliminate(panel, upper, weights, rows):
    n = panel.shape[1] // 128
    sub = lax.broadcasted_iota(jnp.int32, (8, 128), 0)
    weights[...] = jnp.zeros_like(weights)
    pivots = []
    for at in range(0, rows, TALL):
        r = [
            [panel[at + 8 * v : at + 8 * v + 8, 128 * j : 128 * j + 128] for j in range(n)]
            for v in range(TALL // 8)
        ]
        c = [[along(r[v][0], at + k) for k in range(TALL)] for v in range(TALL // 8)]
        scale = [None] * len(r)
        kept = [[None] * n for _ in r]
        for k in range(TALL):
            o, s = divmod(k, 8)
            d = across(c[o][k], s)
            p = 1.0 / d
            root = lax.rsqrt(d)
            pivots.append(d[0:1] * root[0:1])
            scale[o] = p if s == 0 else jnp.where(sub >= s, p, scale[o])
            m = [c[v][k] * p for v in range(len(r))]
            m[o] = jnp.where(sub == s, 0.0, m[o])
            for j in range(n):
                row = across(r[o][j], s)
                now = r[o][j] * root
                kept[o][j] = now if s == 0 else jnp.where(sub >= s, now, kept[o][j])
                for v in range(len(r)):
                    r[v][j] = r[v][j] - m[v] * row
            for q in range(k + 1, TALL):
                row = across(c[o][q], s)
                for v in range(len(r)):
                    c[v][q] = c[v][q] - m[v] * row
        for v in range(len(r)):
            for j in range(n):
                upper[at + 8 * v : at + 8 * v + 8, 128 * j : 128 * j + 128] = kept[v][j]
        if at + TALL == rows:
            break
        for v in range(len(r)):
            for j in range(n):
                weights[at + 8 * v : at + 8 * v + 8, 128 * j : 128 * j + 128] = r[v][j] * scale[v]
        if at:
            weights[at - TALL : at, :] = jnp.zeros((TALL, 128 * n), F32)
        panel[at + TALL : rows, :] -= mm(panel[at + TALL : rows, 0:128], weights[...])
    return pivots


def masked_rows(values, ocean):
    place = lax.broadcasted_iota(jnp.int32, (values.shape[0], 1), 0)
    return jnp.where(place < ocean, values, jnp.zeros_like(values))


def put_gram(ocean, values, out_ref):
    masked = masked_rows(values, ocean)
    row = lax.broadcasted_iota(jnp.int32, (128, 128), 0)
    col = lax.broadcasted_iota(jnp.int32, (128, 128), 1)
    corner = jnp.logical_and(row == 127, col == 0)
    for i in range(4):
        product = lax.dot_general(
            masked[:, 128 * i : 128 * i + 128], masked[:, 128 * i :], TN, preferred_element_type=F32
        )
        for j in range(i, 4):
            block = product[:, 128 * (j - i) : 128 * (j - i) + 128]
            if i == j == 0:
                block = jnp.where(corner, ocean.astype(F32), block)
            at = 16 * AT[i, j]
            for t in range(16):
                tile = at + t
                out_ref[tile // 40, tile % 40 // PIECE, tile % PIECE] = block[8 * t : 8 * t + 8, :]


def reduce_kernel(ocean_ref, values_hbm, both_ref, values, g_ref, sv, from_x, sum_x, from_y, sum_y, from_z, sx, rx, sy, ry, sz, rz, say, ray, sax, rax, sc, rc):
    field = lax.axis_index("field")
    y = lax.axis_index("group")
    row = lax.axis_index("row")
    z, x = row // NX, row % NX

    def at_x(other):
        return (field, y, z * NX + other)

    def at_y(other):
        return (field, other, row)

    def at_z(other):
        return (field, y, other * NX + x)

    partner = (1 - field, y, row)
    xs = [(x + d) % NX for d in range(1, NX)]
    ys = [(y + d) % NY for d in range(1, NY)]
    zs = [(z + d) % NZ for d in range(1, NZ)]
    barrier = pltpu.get_barrier_semaphore()
    everyone = [at_x(o) for o in xs] + [at_y(o) for o in ys] + [at_z(o) for o in zs] + [partner]
    for device in everyone:
        pl.semaphore_signal(barrier, inc=1, device_id=device, device_id_type=MESH)
    load = pltpu.make_async_copy(values_hbm, values, sv)
    load.start()
    load.wait()
    put_gram(ocean_ref[0, 0], values[...], g_ref)
    pl.semaphore_wait(barrier, len(everyone))

    def send(src, dst, s, r, device):
        copy = pltpu.make_async_remote_copy(
            src_ref=src, dst_ref=dst, send_sem=s, recv_sem=r, device_id=device, device_id_type=MESH
        )
        copy.start()
        return copy

    started = []
    copies = [send(g_ref.at[xs[d]], from_x.at[d], sx.at[d], rx.at[d], at_x(xs[d])) for d in range(NX - 1)]
    for copy in copies:
        copy.wait_recv()
    started += copies
    sum_x[...] = g_ref[x] + from_x[0] + from_x[1] + from_x[2]

    copies = [send(sum_x.at[ys[d]], from_y.at[d], sy.at[d], ry.at[d], at_y(ys[d])) for d in range(NY - 1)]
    for copy in copies:
        copy.wait_recv()
    started += copies
    total = sum_x[y]
    for d in range(NY - 1):
        total = total + from_y[d]
    sum_y[...] = total

    copies = [send(sum_y, from_z.at[z], sz.at[d], rz.at[d], at_z(zs[d])) for d in range(NZ - 1)]
    from_z[z] = sum_y[...]
    for copy in copies:
        copy.wait_recv()
    started += copies
    total = from_z[0]
    for other in range(1, NZ):
        total = total + from_z[other]
    mine = both_ref.at[field]
    mine[x, y] = total

    copies = [send(mine.at[x, y], mine.at[x, y], say.at[d], ray.at[d], at_y(ys[d])) for d in range(NY - 1)]
    for copy in copies:
        copy.wait_recv()
    started += copies

    copies = [send(mine.at[x], mine.at[x], sax.at[d], rax.at[d], at_x(xs[d])) for d in range(NX - 1)]
    across_chip = [send(mine.at[x], mine.at[x], sc.at[0], rc.at[0], partner)]
    for d in range(NX - 1):
        copies[d].wait_recv()
        source = (x + NX - 1 - d) % NX
        across_chip.append(send(mine.at[source], mine.at[source], sc.at[d + 1], rc.at[d + 1], partner))
    started += copies
    for copy in across_chip:
        copy.wait_recv()
    for copy in started + across_chip:
        copy.wait_send()


def all_reduced(ocean, values):
    sems = []
    for n in (NX - 1, NY - 1, NZ - 1, NY - 1, NX - 1, NX):
        sems += [pltpu.SemaphoreType.DMA((n,))] * 2
    vm = pl.BlockSpec(memory_space=pltpu.VMEM)
    return pl.pallas_call(
        reduce_kernel,
        out_shape=jax.ShapeDtypeStruct((2, NX, NY, PIECE, 8, 128), F32),
        in_specs=[pl.BlockSpec(memory_space=pltpu.SMEM), pl.BlockSpec(memory_space=pltpu.HBM)],
        out_specs=vm,
        scratch_shapes=[
            pltpu.VMEM((1024, 512), BF16),
            pltpu.VMEM((NX, NY, PIECE, 8, 128), F32),
            pltpu.SemaphoreType.DMA,
            pltpu.VMEM((NX - 1, NY, PIECE, 8, 128), F32),
            pltpu.VMEM((NY, PIECE, 8, 128), F32),
            pltpu.VMEM((NY - 1, PIECE, 8, 128), F32),
            pltpu.VMEM((PIECE, 8, 128), F32),
            pltpu.VMEM((NZ, PIECE, 8, 128), F32),
        ]
        + sems,
        compiler_params=pltpu.CompilerParams(
            collective_id=0, has_side_effects=True, vmem_limit_bytes=32 * 2**20
        ),
    )(ocean, values)


def modes_kernel(ocean_ref, both_ref, st_ref, values_ref, out_ref, strengths_ref, a, u, w, e, eu, st0, fin, g0):
    row = lax.broadcasted_iota(jnp.int32, (128, 128), 0)
    col = lax.broadcasted_iota(jnp.int32, (128, 128), 1)
    corner = jnp.logical_and(row == 127, col == 0)
    which = lax.axis_index("field")

    def scaled(f, at, rate):
        block = both_ref[f, at]
        if at == 0:
            block = jnp.where(corner, block[0:1, 127:128], block)
        return block * rate

    rates = []
    for f in range(2):
        rates.append(1.0 / both_ref[f, 0][127:128, 0:1])
    for i, j in BLOCKS:
        a[128 * i : 128 * i + 128, 128 * j : 128 * j + 128] = scaled(1, AT[i, j], rates[1])
        g0[AT[i, j]] = scaled(0, AT[i, j], rates[0])
    for i in range(4):
        lo, n = 128 * i, 512 - 128 * i
        at = pl.ds(lo, 128)
        eliminate(a.at[at, lo:512], u.at[at, lo:512], w.at[:, 0:n], 128)
        for j in range(i + 1, 4):
            turned = u[lo : lo + 128, 128 * j : 128 * j + 128].T
            a[128 * j : 128 * j + 128, 128 * j : 512] -= mm(turned, u[lo : lo + 128, 128 * j : 512])

    for j in range(4):
        total = None
        for i in range(j + 1):
            block = u[128 * i : 128 * i + 128, 128 * j : 128 * j + 128]
            if i == j:
                block = jnp.where(row <= col, block, 0.0)
            term = mm(st_ref[:, 128 * i : 128 * i + 128], block)
            total = term if total is None else total + term
        e[:, 128 + 128 * j : 256 + 128 * j] = total

    def times_gram(left, block):
        done = []
        for j in range(4):
            total = None
            for i in range(4):
                piece = left[:, 128 * i : 128 * i + 128]
                term = mm(piece, block(i, j)) if i <= j else mm(piece, block(j, i), NT)
                total = term if total is None else total + term
            done.append(total)
        return jnp.concatenate(done, axis=1)

    xt = e[:, 128:640]
    zt = times_gram(xt, lambda i, j: g0[AT[i, j]])
    e[:, 640:1152] = zt
    e[:, 0:128] = jnp.concatenate([mm(xt, zt, NT), jnp.zeros((64, 64), F32)], axis=1)
    eliminate(e, eu, w, 64)
    fin[0] = eu[:, 128:640]
    yt = eu[:, 640:1152]
    ft = times_gram(yt, lambda i, j: scaled(1, AT[i, j], rates[1]))
    e[:, 0:128] = jnp.concatenate([mm(ft, yt, NT), jnp.zeros((64, 64), F32)], axis=1)
    e[:, 128:640] = yt
    pivots = eliminate(e.at[:, 0:640], eu.at[:, 0:640], w.at[:, 0:640], 64)
    fin[1] = eu[:, 128:640]
    lane = lax.broadcasted_iota(jnp.int32, (1, 128), 1)
    line = jnp.zeros((1, 128), F32)
    for k, pivot in enumerate(pivots):
        line = jnp.where(lane == k, pivot, line)
    strengths_ref[...] = line[:, 0:64]
    wh, wl = split(fin[which])
    masked = masked_rows(values_ref[...], ocean_ref[0, 0])
    halves = lax.dot_general(jnp.concatenate([wh, wl], axis=0), masked, NT, preferred_element_type=F32)
    out_ref[...] = halves[0:64] + halves[64:128]


def modes(ocean, both, st, values):
    vm = pl.BlockSpec(memory_space=pltpu.VMEM)
    return pl.pallas_call(
        modes_kernel,
        out_shape=(jax.ShapeDtypeStruct((64, 1024), F32), jax.ShapeDtypeStruct((1, 64), F32)),
        in_specs=[pl.BlockSpec(memory_space=pltpu.SMEM), vm, vm, vm],
        out_specs=(vm, vm),
        scratch_shapes=[
            pltpu.VMEM((512, 512), F32),
            pltpu.VMEM((512, 512), F32),
            pltpu.VMEM((128, 1152), F32),
            pltpu.VMEM((64, 1152), F32),
            pltpu.VMEM((64, 1152), F32),
            pltpu.VMEM((64, 512), F32),
            pltpu.VMEM((2, 64, 512), F32),
            pltpu.VMEM((10, 128, 128), F32),
        ],
        compiler_params=pltpu.CompilerParams(vmem_limit_bytes=48 * 2**20),
    )(ocean, both.reshape(2, 10, 128, 128), st, values)


def per_device(anomalies, valid_rows, start_basis):
    values = anomalies[0]
    both = all_reduced(valid_rows, values)
    patterns, strengths = modes(valid_rows, both, start_basis.T, values)
    return patterns.T[None], strengths.reshape(64)


def solution(mesh):
    shards = ("group", "row")
    in_specs = (P("field", shards, None), P("field", shards), P())
    out_specs = (P("field", shards, None), P())
    return jax.shard_map(
        per_device, mesh=mesh, in_specs=in_specs, out_specs=out_specs, check_vma=False
    )
```

```python
import functools

import jax
import jax.numpy as jnp
from jax import lax
from jax.experimental import pallas as pl
from jax.experimental.pallas import tpu as pltpu
from jax.sharding import PartitionSpec as P

F32, BF16 = jnp.float32, jnp.bfloat16
NN = (((1,), (0,)), ((), ()))
NT = (((1,), (1,)), ((), ()))
TN = (((0,), (0,)), ((), ()))
MESH = pl.DeviceIdType.MESH
NX = 4
SIZE = {"x": NX, "y": 8, "z": 8}
FAR = {4: (1, 3, 2), 8: (1, 7, 2, 6, 3, 5, 4)}
STREAMS = (("x", "y", "z", 64), ("y", "x", "z", 32), ("z", "x", "y", 64))
TALL = 16
BLOCKS = [(i, j) for i in range(4) for j in range(i, 4)]
AT = {pair: at for at, pair in enumerate(BLOCKS)}


def split(x):
    hi = x.astype(BF16)
    return hi, (x - hi.astype(F32)).astype(BF16)


def mm(a, b, dims=NN):
    ah, al = split(a)
    bh, bl = split(b)
    dot = functools.partial(lax.dot_general, dimension_numbers=dims, preferred_element_type=F32)
    return dot(ah, bh) + (dot(ah, bl) + dot(al, bh))


def across(x, k):
    return jnp.broadcast_to(x[k : k + 1, :], (8, 128))


def along(x, k):
    return jnp.broadcast_to(x[:, k : k + 1], (8, 128))


def eliminate(panel, upper, weights, rows):
    n = panel.shape[1] // 128
    sub = lax.broadcasted_iota(jnp.int32, (8, 128), 0)
    weights[...] = jnp.zeros_like(weights)
    pivots = []
    for at in range(0, rows, TALL):
        r = [
            [panel[at + 8 * v : at + 8 * v + 8, 128 * j : 128 * j + 128] for j in range(n)]
            for v in range(TALL // 8)
        ]
        c = [[along(r[v][0], at + k) for k in range(TALL)] for v in range(TALL // 8)]
        scale = [None] * len(r)
        kept = [[None] * n for _ in r]
        for k in range(TALL):
            o, s = divmod(k, 8)
            d = across(c[o][k], s)
            p = 1.0 / d
            root = lax.rsqrt(d)
            pivots.append(d[0:1] * root[0:1])
            scale[o] = p if s == 0 else jnp.where(sub >= s, p, scale[o])
            m = [c[v][k] * p for v in range(len(r))]
            m[o] = jnp.where(sub == s, 0.0, m[o])
            for j in range(n):
                row = across(r[o][j], s)
                now = r[o][j] * root
                kept[o][j] = now if s == 0 else jnp.where(sub >= s, now, kept[o][j])
                for v in range(len(r)):
                    r[v][j] = r[v][j] - m[v] * row
            for q in range(k + 1, TALL):
                row = across(c[o][q], s)
                for v in range(len(r)):
                    c[v][q] = c[v][q] - m[v] * row
        for v in range(len(r)):
            for j in range(n):
                upper[at + 8 * v : at + 8 * v + 8, 128 * j : 128 * j + 128] = kept[v][j]
        if at + TALL == rows:
            break
        for v in range(len(r)):
            for j in range(n):
                weights[at + 8 * v : at + 8 * v + 8, 128 * j : 128 * j + 128] = r[v][j] * scale[v]
        if at:
            weights[at - TALL : at, :] = jnp.zeros((TALL, 128 * n), F32)
        panel[at + TALL : rows, :] -= mm(panel[at + TALL : rows, 0:128], weights[...])
    return pivots


def masked_rows(values, ocean):
    place = lax.broadcasted_iota(jnp.int32, (values.shape[0], 1), 0)
    return jnp.where(place < ocean, values, jnp.zeros_like(values))


def put_gram(ocean, values, out_ref):
    masked = masked_rows(values, ocean)
    row = lax.broadcasted_iota(jnp.int32, (128, 128), 0)
    col = lax.broadcasted_iota(jnp.int32, (128, 128), 1)
    corner = jnp.logical_and(row == 127, col == 0)
    for i in range(4):
        product = lax.dot_general(
            masked[:, 128 * i : 128 * i + 128], masked[:, 128 * i :], TN, preferred_element_type=F32
        )
        for j in range(i, 4):
            block = product[:, 128 * (j - i) : 128 * (j - i) + 128]
            if i == j == 0:
                block = jnp.where(corner, ocean.astype(F32), block)
            out_ref[16 * AT[i, j] : 16 * AT[i, j] + 16] = block.reshape(16, 8, 128)


class Stream:
    SCRATCH = 17

    def __init__(self, spec, start, refs, me, device, partner, own, mine):
        self.a, self.b, self.c, tiles = spec
        self.na, self.nb, self.nc = SIZE[self.a], SIZE[self.b], SIZE[self.c]
        self.unit = tiles // (self.na * self.nb)
        self.start = start
        self.from_a, self.sum_a, self.from_b, self.sum_b, self.from_c = refs[:5]
        self.sems = refs[5:]
        self.me, self.device, self.partner = me, device, partner
        self.own, self.mine = own, mine
        self.started, self.live, self.over = [], [], []

    @staticmethod
    def scratch(spec):
        a, b, c, tiles = spec
        na, nb, nc = SIZE[a], SIZE[b], SIZE[c]
        unit = tiles // (na * nb)
        shapes = [(na - 1, nb * unit), (nb * unit,), (nb - 1, unit), (unit,), (nc, unit)]
        sems = []
        for n in (na - 1, nb - 1, nc - 1, nb - 1, na - 1, na):
            sems += [pltpu.SemaphoreType.DMA((n,))] * 2
        return [pltpu.VMEM((*shape, 8, 128), F32) for shape in shapes] + sems

    def part(self, i):
        return pl.ds(self.start + i * (self.nb * self.unit), self.nb * self.unit)

    def piece(self, i, j):
        return pl.ds(self.start + (i * self.nb + j) * self.unit, self.unit)

    def send(self, phase, k, src, dst, device):
        copy = pltpu.make_async_remote_copy(
            src_ref=src,
            dst_ref=dst,
            send_sem=self.sems[2 * phase].at[k],
            recv_sem=self.sems[2 * phase + 1].at[k],
            device_id=device,
            device_id_type=MESH,
        )
        copy.start()
        self.started.append(copy)
        return copy

    def to_all(self, phase, axis, src, dst):
        size = SIZE[axis]
        self.live = []
        for k, far in enumerate(FAR[size]):
            other = (self.me[axis] + far) % size
            self.live.append(self.send(phase, k, src(other), dst(k), self.device[axis](other)))

    def received(self):
        for copy in self.live:
            copy.wait_recv()

    def scatter_a(self):
        self.to_all(0, self.a, lambda o: self.own.at[self.part(o)], lambda k: self.from_a.at[k])

    def scatter_b(self):
        self.received()
        total = self.own[self.part(self.me[self.a])]
        for k in range(self.na - 1):
            total = total + self.from_a[k]
        self.sum_a[...] = total
        unit = self.unit
        self.to_all(
            1, self.b, lambda o: self.sum_a.at[pl.ds(o * unit, unit)], lambda k: self.from_b.at[k]
        )

    def exchange_c(self):
        self.received()
        total = self.sum_a[pl.ds(self.me[self.b] * self.unit, self.unit)]
        for k in range(self.nb - 1):
            total = total + self.from_b[k]
        self.sum_b[...] = total
        place = self.me[self.c]
        self.to_all(2, self.c, lambda o: self.sum_b, lambda k: self.from_c.at[place])
        self.from_c[place] = total

    def gather_b(self):
        self.received()
        total = self.from_c[0]
        for k in range(1, self.nc):
            total = total + self.from_c[k]
        at = self.piece(self.me[self.a], self.me[self.b])
        self.mine[at] = total
        self.to_all(3, self.b, lambda o: self.mine.at[at], lambda k: self.mine.at[at])

    def gather_a(self):
        self.received()
        at = self.part(self.me[self.a])
        self.to_all(4, self.a, lambda o: self.mine.at[at], lambda k: self.mine.at[at])
        self.over = [self.send(5, 0, self.mine.at[at], self.mine.at[at], self.partner)]

    def hand_over(self):
        gathered = self.live
        for k, far in enumerate(FAR[self.na]):
            gathered[k].wait_recv()
            at = self.part((self.me[self.a] + self.na - far) % self.na)
            self.over.append(self.send(5, k + 1, self.mine.at[at], self.mine.at[at], self.partner))

    def close(self):
        for copy in self.over:
            copy.wait_recv()
        for copy in self.started:
            copy.wait_send()


STEPS = ("scatter_a", "scatter_b", "exchange_c", "gather_b", "gather_a", "hand_over", "close")


def reduce_kernel(ocean_ref, values_hbm, both_ref, values, own, loaded, *refs):
    field = lax.axis_index("field")
    y = lax.axis_index("group")
    row = lax.axis_index("row")
    z, x = row // NX, row % NX
    me = {"x": x, "y": y, "z": z}
    device = {
        "x": lambda other: (field, y, z * NX + other),
        "y": lambda other: (field, other, row),
        "z": lambda other: (field, y, other * NX + x),
    }
    partner = (1 - field, y, row)
    barrier = pltpu.get_barrier_semaphore()
    everyone = [partner]
    for axis, size in SIZE.items():
        everyone += [device[axis]((me[axis] + far) % size) for far in FAR[size]]
    for other in everyone:
        pl.semaphore_signal(barrier, inc=1, device_id=other, device_id_type=MESH)
    load = pltpu.make_async_copy(values_hbm, values, loaded)
    load.start()
    load.wait()
    put_gram(ocean_ref[0, 0], values[...], own)
    pl.semaphore_wait(barrier, len(everyone))

    streams, start = [], 0
    for k, spec in enumerate(STREAMS):
        mine = refs[Stream.SCRATCH * k : Stream.SCRATCH * (k + 1)]
        streams.append(Stream(spec, start, mine, me, device, partner, own, both_ref.at[field]))
        start += spec[3]
    for step in STEPS:
        for stream in streams:
            getattr(stream, step)()


def all_reduced(ocean, values):
    scratch = []
    for spec in STREAMS:
        scratch += Stream.scratch(spec)
    return pl.pallas_call(
        reduce_kernel,
        out_shape=jax.ShapeDtypeStruct((2, 160, 8, 128), F32),
        in_specs=[pl.BlockSpec(memory_space=pltpu.SMEM), pl.BlockSpec(memory_space=pltpu.HBM)],
        out_specs=pl.BlockSpec(memory_space=pltpu.VMEM),
        scratch_shapes=[
            pltpu.VMEM((1024, 512), BF16),
            pltpu.VMEM((160, 8, 128), F32),
            pltpu.SemaphoreType.DMA,
        ]
        + scratch,
        compiler_params=pltpu.CompilerParams(
            collective_id=0, has_side_effects=True, vmem_limit_bytes=32 * 2**20
        ),
    )(ocean, values)


def modes_kernel(ocean_ref, both_ref, st_ref, values_ref, out_ref, strengths_ref, a, u, w, e, eu, st0, fin, g0):
    row = lax.broadcasted_iota(jnp.int32, (128, 128), 0)
    col = lax.broadcasted_iota(jnp.int32, (128, 128), 1)
    corner = jnp.logical_and(row == 127, col == 0)
    which = lax.axis_index("field")

    def scaled(f, at, rate):
        block = both_ref[f, at]
        if at == 0:
            block = jnp.where(corner, block[0:1, 127:128], block)
        return block * rate

    rates = []
    for f in range(2):
        rates.append(1.0 / both_ref[f, 0][127:128, 0:1])
    for i, j in BLOCKS:
        a[128 * i : 128 * i + 128, 128 * j : 128 * j + 128] = scaled(1, AT[i, j], rates[1])
        g0[AT[i, j]] = scaled(0, AT[i, j], rates[0])
    for i in range(4):
        lo, n = 128 * i, 512 - 128 * i
        at = pl.ds(lo, 128)
        eliminate(a.at[at, lo:512], u.at[at, lo:512], w.at[:, 0:n], 128)
        for j in range(i + 1, 4):
            turned = u[lo : lo + 128, 128 * j : 128 * j + 128].T
            a[128 * j : 128 * j + 128, 128 * j : 512] -= mm(turned, u[lo : lo + 128, 128 * j : 512])

    for j in range(4):
        total = None
        for i in range(j + 1):
            block = u[128 * i : 128 * i + 128, 128 * j : 128 * j + 128]
            if i == j:
                block = jnp.where(row <= col, block, 0.0)
            term = mm(st_ref[:, 128 * i : 128 * i + 128], block)
            total = term if total is None else total + term
        e[:, 128 + 128 * j : 256 + 128 * j] = total

    def times_gram(left, block):
        done = []
        for j in range(4):
            total = None
            for i in range(4):
                piece = left[:, 128 * i : 128 * i + 128]
                term = mm(piece, block(i, j)) if i <= j else mm(piece, block(j, i), NT)
                total = term if total is None else total + term
            done.append(total)
        return jnp.concatenate(done, axis=1)

    xt = e[:, 128:640]
    zt = times_gram(xt, lambda i, j: g0[AT[i, j]])
    e[:, 640:1152] = zt
    e[:, 0:128] = jnp.concatenate([mm(xt, zt, NT), jnp.zeros((64, 64), F32)], axis=1)
    eliminate(e, eu, w, 64)
    fin[0] = eu[:, 128:640]
    yt = eu[:, 640:1152]
    ft = times_gram(yt, lambda i, j: scaled(1, AT[i, j], rates[1]))
    e[:, 0:128] = jnp.concatenate([mm(ft, yt, NT), jnp.zeros((64, 64), F32)], axis=1)
    e[:, 128:640] = yt
    pivots = eliminate(e.at[:, 0:640], eu.at[:, 0:640], w.at[:, 0:640], 64)
    fin[1] = eu[:, 128:640]
    lane = lax.broadcasted_iota(jnp.int32, (1, 128), 1)
    line = jnp.zeros((1, 128), F32)
    for k, pivot in enumerate(pivots):
        line = jnp.where(lane == k, pivot, line)
    strengths_ref[...] = line[:, 0:64]
    wh, wl = split(fin[which])
    masked = masked_rows(values_ref[...], ocean_ref[0, 0])
    halves = lax.dot_general(jnp.concatenate([wh, wl], axis=0), masked, NT, preferred_element_type=F32)
    out_ref[...] = halves[0:64] + halves[64:128]


def modes(ocean, both, st, values):
    vm = pl.BlockSpec(memory_space=pltpu.VMEM)
    return pl.pallas_call(
        modes_kernel,
        out_shape=(jax.ShapeDtypeStruct((64, 1024), F32), jax.ShapeDtypeStruct((1, 64), F32)),
        in_specs=[pl.BlockSpec(memory_space=pltpu.SMEM), vm, vm, vm],
        out_specs=(vm, vm),
        scratch_shapes=[
            pltpu.VMEM((512, 512), F32),
            pltpu.VMEM((512, 512), F32),
            pltpu.VMEM((128, 1152), F32),
            pltpu.VMEM((64, 1152), F32),
            pltpu.VMEM((64, 1152), F32),
            pltpu.VMEM((64, 512), F32),
            pltpu.VMEM((2, 64, 512), F32),
            pltpu.VMEM((10, 128, 128), F32),
        ],
        compiler_params=pltpu.CompilerParams(vmem_limit_bytes=48 * 2**20),
    )(ocean, both.reshape(2, 10, 128, 128), st, values)


def per_device(anomalies, valid_rows, start_basis):
    values = anomalies[0]
    both = all_reduced(valid_rows, values)
    patterns, strengths = modes(valid_rows, both, start_basis.T, values)
    return patterns.T[None], strengths.reshape(64)


def solution(mesh):
    shards = ("group", "row")
    in_specs = (P("field", shards, None), P("field", shards), P())
    out_specs = (P("field", shards, None), P())
    return jax.shard_map(
        per_device, mesh=mesh, in_specs=in_specs, out_specs=out_specs, check_vma=False
    )
```

```python
import functools

import jax
import jax.numpy as jnp
from jax import lax
from jax.experimental import pallas as pl
from jax.experimental.pallas import tpu as pltpu
from jax.sharding import PartitionSpec as P

F32, BF16 = jnp.float32, jnp.bfloat16
NN = (((1,), (0,)), ((), ()))
NT = (((1,), (1,)), ((), ()))
TN = (((0,), (0,)), ((), ()))
MESH = pl.DeviceIdType.MESH
NX = 4
SIZE = {"x": NX, "y": 8, "z": 8}
FAR = {4: (1, 3, 2), 8: (1, 7, 2, 6, 3, 5, 4)}
STREAMS = (("x", "y", "z", 64), ("y", "x", "z", 32), ("z", "x", "y", 64))
TALL = 16
BLOCKS = [(i, j) for i in range(4) for j in range(i, 4)]
AT = {pair: at for at, pair in enumerate(BLOCKS)}


def split(x):
    hi = x.astype(BF16)
    return hi, (x - hi.astype(F32)).astype(BF16)


def mm(a, b, dims=NN):
    ah, al = split(a)
    bh, bl = split(b)
    dot = functools.partial(lax.dot_general, dimension_numbers=dims, preferred_element_type=F32)
    return dot(ah, bh) + (dot(ah, bl) + dot(al, bh))


def across(x, k):
    return jnp.broadcast_to(x[k : k + 1, :], (8, 128))


def along(x, k):
    return jnp.broadcast_to(x[:, k : k + 1], (8, 128))


def eliminate(panel, upper, weights, rows):
    n = panel.shape[1] // 128
    sub = lax.broadcasted_iota(jnp.int32, (8, 128), 0)
    weights[...] = jnp.zeros_like(weights)
    pivots = []
    for at in range(0, rows, TALL):
        r = [
            [panel[at + 8 * v : at + 8 * v + 8, 128 * j : 128 * j + 128] for j in range(n)]
            for v in range(TALL // 8)
        ]
        c = [[along(r[v][0], at + k) for k in range(TALL)] for v in range(TALL // 8)]
        scale = [None] * len(r)
        kept = [[None] * n for _ in r]
        for k in range(TALL):
            o, s = divmod(k, 8)
            d = across(c[o][k], s)
            p = 1.0 / d
            root = lax.rsqrt(d)
            pivots.append(d[0:1] * root[0:1])
            scale[o] = p if s == 0 else jnp.where(sub >= s, p, scale[o])
            m = [c[v][k] * p for v in range(len(r))]
            m[o] = jnp.where(sub == s, 0.0, m[o])
            for j in range(n):
                row = across(r[o][j], s)
                now = r[o][j] * root
                kept[o][j] = now if s == 0 else jnp.where(sub >= s, now, kept[o][j])
                for v in range(len(r)):
                    r[v][j] = r[v][j] - m[v] * row
            for q in range(k + 1, TALL):
                row = across(c[o][q], s)
                for v in range(len(r)):
                    c[v][q] = c[v][q] - m[v] * row
        for v in range(len(r)):
            for j in range(n):
                upper[at + 8 * v : at + 8 * v + 8, 128 * j : 128 * j + 128] = kept[v][j]
        if at + TALL == rows:
            break
        for v in range(len(r)):
            for j in range(n):
                weights[at + 8 * v : at + 8 * v + 8, 128 * j : 128 * j + 128] = r[v][j] * scale[v]
        if at:
            weights[at - TALL : at, :] = jnp.zeros((TALL, 128 * n), F32)
        panel[at + TALL : rows, :] -= mm(panel[at + TALL : rows, 0:128], weights[...])
    return pivots


def masked_rows(values, ocean):
    place = lax.broadcasted_iota(jnp.int32, (values.shape[0], 1), 0)
    return jnp.where(place < ocean, values, jnp.zeros_like(values))


def put_gram(ocean, values, out_ref):
    masked = masked_rows(values, ocean)
    row = lax.broadcasted_iota(jnp.int32, (128, 128), 0)
    col = lax.broadcasted_iota(jnp.int32, (128, 128), 1)
    corner = jnp.logical_and(row == 127, col == 0)
    for i in range(4):
        product = lax.dot_general(
            masked[:, 128 * i : 128 * i + 128], masked[:, 128 * i :], TN, preferred_element_type=F32
        )
        for j in range(i, 4):
            block = product[:, 128 * (j - i) : 128 * (j - i) + 128]
            if i == j == 0:
                block = jnp.where(corner, ocean.astype(F32), block)
            out_ref[16 * AT[i, j] : 16 * AT[i, j] + 16] = block.reshape(16, 8, 128)


class Stream:
    SCRATCH = 17

    def __init__(self, spec, start, refs, me, device, partner, own, mine):
        self.a, self.b, self.c, tiles = spec
        self.na, self.nb, self.nc = SIZE[self.a], SIZE[self.b], SIZE[self.c]
        self.unit = tiles // (self.na * self.nb)
        self.start = start
        self.from_a, self.sum_a, self.from_b, self.sum_b, self.from_c = refs[:5]
        self.sems = refs[5:]
        self.me, self.device, self.partner = me, device, partner
        self.own, self.mine = own, mine
        self.started, self.live = [], []

    @staticmethod
    def scratch(spec):
        a, b, c, tiles = spec
        na, nb, nc = SIZE[a], SIZE[b], SIZE[c]
        unit = tiles // (na * nb)
        shapes = [(na - 1, nb * unit), (nb * unit,), (nb - 1, unit), (unit,), (nc, unit)]
        sems = []
        for n in (na - 1, nb - 1, nc - 1, nb - 1, na - 1, na):
            sems += [pltpu.SemaphoreType.DMA((n,))] * 2
        return [pltpu.VMEM((*shape, 8, 128), F32) for shape in shapes] + sems

    def part(self, i):
        return pl.ds(self.start + i * (self.nb * self.unit), self.nb * self.unit)

    def piece(self, i, j):
        return pl.ds(self.start + (i * self.nb + j) * self.unit, self.unit)

    def send(self, phase, k, src, dst, device):
        copy = pltpu.make_async_remote_copy(
            src_ref=src,
            dst_ref=dst,
            send_sem=self.sems[2 * phase].at[k],
            recv_sem=self.sems[2 * phase + 1].at[k],
            device_id=device,
            device_id_type=MESH,
        )
        copy.start()
        self.started.append(copy)
        return copy

    def to_all(self, phase, axis, src, dst):
        size = SIZE[axis]
        self.live = []
        for k, far in enumerate(FAR[size]):
            other = (self.me[axis] + far) % size
            self.live.append(self.send(phase, k, src(other), dst(k), self.device[axis](other)))

    def received(self):
        for copy in self.live:
            copy.wait_recv()

    def scatter_a(self):
        self.to_all(0, self.a, lambda o: self.own.at[self.part(o)], lambda k: self.from_a.at[k])

    def scatter_b(self):
        self.received()
        total = self.own[self.part(self.me[self.a])]
        for k in range(self.na - 1):
            total = total + self.from_a[k]
        self.sum_a[...] = total
        unit = self.unit
        self.to_all(
            1, self.b, lambda o: self.sum_a.at[pl.ds(o * unit, unit)], lambda k: self.from_b.at[k]
        )

    def exchange_c(self):
        self.received()
        total = self.sum_a[pl.ds(self.me[self.b] * self.unit, self.unit)]
        for k in range(self.nb - 1):
            total = total + self.from_b[k]
        self.sum_b[...] = total
        place = self.me[self.c]
        self.to_all(2, self.c, lambda o: self.sum_b, lambda k: self.from_c.at[place])
        self.from_c[place] = total

    def gather_b(self):
        self.received()
        total = self.from_c[0]
        for k in range(1, self.nc):
            total = total + self.from_c[k]
        at = self.piece(self.me[self.a], self.me[self.b])
        self.mine[at] = total
        self.to_all(3, self.b, lambda o: self.mine.at[at], lambda k: self.mine.at[at])

    def gather_a(self):
        self.received()
        at = self.part(self.me[self.a])
        self.to_all(4, self.a, lambda o: self.mine.at[at], lambda k: self.mine.at[at])

    def over(self, k):
        far = (0, *FAR[self.na])[k]
        at = self.part((self.me[self.a] + self.na - far) % self.na)
        return pltpu.make_async_remote_copy(
            src_ref=self.mine.at[at],
            dst_ref=self.mine.at[at],
            send_sem=self.sems[10].at[k],
            recv_sem=self.sems[11].at[k],
            device_id=self.partner,
            device_id_type=MESH,
        )

    def hand_over(self):
        for k in range(self.na):
            if k:
                self.live[k - 1].wait_recv()
            self.over(k).start()

    def taken_over(self, theirs):
        for k in range(self.na):
            far = (0, *FAR[self.na])[k]
            at = self.part((self.me[self.a] + self.na - far) % self.na)
            pltpu.make_async_remote_copy(
                src_ref=theirs.at[at],
                dst_ref=theirs.at[at],
                send_sem=self.sems[10].at[k],
                recv_sem=self.sems[11].at[k],
                device_id=self.partner,
                device_id_type=MESH,
            ).wait_recv()


def times_gram(left, block):
    done = []
    for j in range(4):
        total = None
        for i in range(4):
            piece = left[:, 128 * i : 128 * i + 128]
            term = mm(piece, block(i, j)) if i <= j else mm(piece, block(j, i), NT)
            total = term if total is None else total + term
        done.append(total)
    return jnp.concatenate(done, axis=1)


def square(product):
    return jnp.concatenate([product, jnp.zeros_like(product)], axis=1)


def whole_kernel(
    ocean_ref, st_ref, values_hbm, out_ref, strengths_ref,
    values, own, both, a, u, w, e, eu, fin, xt, line, loaded, go, sx, rx, sl, rl, *refs
):
    field = lax.axis_index("field")
    y = lax.axis_index("group")
    row = lax.axis_index("row")
    z, x = row // NX, row % NX
    me = {"x": x, "y": y, "z": z}
    device = {
        "x": lambda other: (field, y, z * NX + other),
        "y": lambda other: (field, other, row),
        "z": lambda other: (field, y, other * NX + x),
    }
    partner = (1 - field, y, row)
    first, second = field == 0, field == 1
    barrier = pltpu.get_barrier_semaphore()
    everyone = [partner]
    for axis, size in SIZE.items():
        everyone += [device[axis]((me[axis] + far) % size) for far in FAR[size]]
    for other in everyone:
        pl.semaphore_signal(barrier, inc=1, device_id=other, device_id_type=MESH)
    load = pltpu.make_async_copy(values_hbm, values, loaded)
    load.start()
    load.wait()
    put_gram(ocean_ref[0, 0], values[...], own)
    pl.semaphore_wait(barrier, len(everyone))

    streams, start = [], 0
    for k, spec in enumerate(STREAMS):
        mine = refs[Stream.SCRATCH * k : Stream.SCRATCH * (k + 1)]
        streams.append(Stream(spec, start, mine, me, device, partner, own, both.at[field]))
        start += spec[3]

    @pl.when(first)
    def _():
        pl.semaphore_wait(go, 1)

    for stream in streams:
        stream.scatter_a()
    for stream in streams:
        stream.scatter_b()

    @pl.when(second)
    def _():
        pl.semaphore_signal(go, inc=1, device_id=partner, device_id_type=MESH)

    for step in ("exchange_c", "gather_b", "gather_a"):
        for stream in streams:
            getattr(stream, step)()

    line_row = lax.broadcasted_iota(jnp.int32, (128, 128), 0)
    line_col = lax.broadcasted_iota(jnp.int32, (128, 128), 1)
    corner = jnp.logical_and(line_row == 127, line_col == 0)

    def raw(f, at):
        return both[f, 16 * at : 16 * at + 16].reshape(128, 128)

    def scaled(f, at, rate):
        block = raw(f, at)
        if at == 0:
            block = jnp.where(corner, block[0:1, 127:128], block)
        return block * rate

    def rate_of(f):
        return 1.0 / raw(f, 0)[127:128, 0:1]

    def across_chip(j):
        return pltpu.make_async_remote_copy(
            src_ref=xt.at[j], dst_ref=xt.at[j], send_sem=sx.at[j], recv_sem=rx.at[j],
            device_id=partner, device_id_type=MESH,
        )

    def strengths_across():
        return pltpu.make_async_remote_copy(
            src_ref=line, dst_ref=line, send_sem=sl, recv_sem=rl,
            device_id=partner, device_id_type=MESH,
        )

    @pl.when(first)
    def _():
        for stream in streams:
            stream.hand_over()
        for j in range(4):
            across_chip(j).wait_recv()

    @pl.when(second)
    def _():
        for stream in streams:
            stream.received()
        rate = rate_of(1)
        for i, j in BLOCKS:
            a[128 * i : 128 * i + 128, 128 * j : 128 * j + 128] = scaled(1, AT[i, j], rate)
        for i in range(4):
            lo, n = 128 * i, 512 - 128 * i
            at = pl.ds(lo, 128)
            eliminate(a.at[at, lo:512], u.at[at, lo:512], w.at[:, 0:n], 128)
            for j in range(i + 1, 4):
                turned = u[lo : lo + 128, 128 * j : 128 * j + 128].T
                a[128 * j : 128 * j + 128, 128 * j : 512] -= mm(turned, u[lo : lo + 128, 128 * j : 512])
            total = None
            for k in range(i + 1):
                block = u[128 * k : 128 * k + 128, lo : lo + 128]
                if k == i:
                    block = jnp.where(line_row <= line_col, block, 0.0)
                term = mm(st_ref[:, 128 * k : 128 * k + 128], block)
                total = term if total is None else total + term
            xt[i] = total
            across_chip(i).start()
        for stream in streams:
            stream.taken_over(both.at[0])

    rate0 = rate_of(0)
    left = jnp.concatenate([xt[j] for j in range(4)], axis=1)
    zt = times_gram(left, lambda i, j: scaled(0, AT[i, j], rate0))
    e[:, 128:640] = left
    e[:, 640:1152] = zt
    e[:, 0:128] = square(mm(left, zt, NT))
    eliminate(e, eu, w, 64)

    @pl.when(first)
    def _():
        fin[...] = eu[:, 128:640]

    @pl.when(second)
    def _():
        rate1 = rate_of(1)
        yt = eu[:, 640:1152]
        ft = times_gram(yt, lambda i, j: scaled(1, AT[i, j], rate1))
        e[:, 0:128] = square(mm(ft, yt, NT))
        e[:, 128:640] = yt
        pivots = eliminate(e.at[:, 0:640], eu.at[:, 0:640], w.at[:, 0:640], 64)
        fin[...] = eu[:, 128:640]
        lane = lax.broadcasted_iota(jnp.int32, (8, 128), 1)
        drawn = jnp.zeros((8, 128), F32)
        for k, pivot in enumerate(pivots):
            drawn = jnp.where(lane == k, pivot, drawn)
        line[...] = drawn
        strengths_across().start()

    wh, wl = split(fin[...])
    masked = masked_rows(values[...], ocean_ref[0, 0])
    halves = lax.dot_general(jnp.concatenate([wh, wl], axis=0), masked, NT, preferred_element_type=F32)
    out_ref[...] = halves[0:64] + halves[64:128]

    @pl.when(first)
    def _():
        strengths_across().wait_recv()
        for stream in streams:
            for k in range(stream.na):
                stream.over(k).wait_send()

    @pl.when(second)
    def _():
        strengths_across().wait_send()
        for j in range(4):
            across_chip(j).wait_send()

    for stream in streams:
        for copy in stream.started:
            copy.wait_send()
    strengths_ref[...] = line[0:1, 0:64]


def whole(ocean, st, values):
    scratch = []
    for spec in STREAMS:
        scratch += Stream.scratch(spec)
    vm = pl.BlockSpec(memory_space=pltpu.VMEM)
    return pl.pallas_call(
        whole_kernel,
        out_shape=(jax.ShapeDtypeStruct((64, 1024), F32), jax.ShapeDtypeStruct((1, 64), F32)),
        in_specs=[pl.BlockSpec(memory_space=pltpu.SMEM), vm, pl.BlockSpec(memory_space=pltpu.HBM)],
        out_specs=(vm, vm),
        scratch_shapes=[
            pltpu.VMEM((1024, 512), BF16),
            pltpu.VMEM((160, 8, 128), F32),
            pltpu.VMEM((2, 160, 8, 128), F32),
            pltpu.VMEM((512, 512), F32),
            pltpu.VMEM((512, 512), F32),
            pltpu.VMEM((128, 1152), F32),
            pltpu.VMEM((64, 1152), F32),
            pltpu.VMEM((64, 1152), F32),
            pltpu.VMEM((64, 512), F32),
            pltpu.VMEM((4, 64, 128), F32),
            pltpu.VMEM((8, 128), F32),
            pltpu.SemaphoreType.DMA,
            pltpu.SemaphoreType.REGULAR,
            pltpu.SemaphoreType.DMA((4,)),
            pltpu.SemaphoreType.DMA((4,)),
            pltpu.SemaphoreType.DMA,
            pltpu.SemaphoreType.DMA,
        ]
        + scratch,
        compiler_params=pltpu.CompilerParams(
            collective_id=0, has_side_effects=True, vmem_limit_bytes=60 * 2**20
        ),
    )(ocean, st, values)


def per_device(anomalies, valid_rows, start_basis):
    patterns, strengths = whole(valid_rows, start_basis.T, anomalies[0])
    return patterns.T[None], strengths.reshape(64)


def solution(mesh):
    shards = ("group", "row")
    in_specs = (P("field", shards, None), P("field", shards), P())
    out_specs = (P("field", shards, None), P())
    return jax.shard_map(
        per_device, mesh=mesh, in_specs=in_specs, out_specs=out_specs, check_vma=False
    )
```

```python
import functools

import jax
import jax.numpy as jnp
from jax import lax
from jax.experimental import pallas as pl
from jax.experimental.pallas import tpu as pltpu
from jax.sharding import PartitionSpec as P

F32, BF16 = jnp.float32, jnp.bfloat16
NN = (((1,), (0,)), ((), ()))
NT = (((1,), (1,)), ((), ()))
TN = (((0,), (0,)), ((), ()))
MESH = pl.DeviceIdType.MESH
NX = 4
SIZE = {"x": NX, "y": 8, "z": 8}
FAR = {4: (1, 3, 2), 8: (1, 7, 2, 6, 3, 5, 4)}
STREAMS = (("x", "y", "z", 64), ("z", "x", "y", 32), ("x", "z", "y", 64))
TALL = 16
BLOCKS = [(i, j) for i in range(4) for j in range(i, 4)]
AT = {pair: at for at, pair in enumerate(BLOCKS)}


def split(x):
    hi = x.astype(BF16)
    return hi, (x - hi.astype(F32)).astype(BF16)


def mm(a, b, dims=NN):
    ah, al = split(a)
    bh, bl = split(b)
    dot = functools.partial(lax.dot_general, dimension_numbers=dims, preferred_element_type=F32)
    return dot(ah, bh) + (dot(ah, bl) + dot(al, bh))


def across(x, k):
    return jnp.broadcast_to(x[k : k + 1, :], (8, 128))


def along(x, k):
    return jnp.broadcast_to(x[:, k : k + 1], (8, 128))


def eliminate(panel, upper, weights, rows):
    n = panel.shape[1] // 128
    sub = lax.broadcasted_iota(jnp.int32, (8, 128), 0)
    weights[...] = jnp.zeros_like(weights)
    pivots = []
    for at in range(0, rows, TALL):
        r = [
            [panel[at + 8 * v : at + 8 * v + 8, 128 * j : 128 * j + 128] for j in range(n)]
            for v in range(TALL // 8)
        ]
        c = [[along(r[v][0], at + k) for k in range(TALL)] for v in range(TALL // 8)]
        scale = [None] * len(r)
        kept = [[None] * n for _ in r]
        for k in range(TALL):
            o, s = divmod(k, 8)
            d = across(c[o][k], s)
            p = 1.0 / d
            root = lax.rsqrt(d)
            pivots.append(d[0:1] * root[0:1])
            scale[o] = p if s == 0 else jnp.where(sub >= s, p, scale[o])
            m = [c[v][k] * p for v in range(len(r))]
            m[o] = jnp.where(sub == s, 0.0, m[o])
            for j in range(n):
                row = across(r[o][j], s)
                now = r[o][j] * root
                kept[o][j] = now if s == 0 else jnp.where(sub >= s, now, kept[o][j])
                for v in range(len(r)):
                    r[v][j] = r[v][j] - m[v] * row
            for q in range(k + 1, TALL):
                row = across(c[o][q], s)
                for v in range(len(r)):
                    c[v][q] = c[v][q] - m[v] * row
        for v in range(len(r)):
            for j in range(n):
                upper[at + 8 * v : at + 8 * v + 8, 128 * j : 128 * j + 128] = kept[v][j]
        if at + TALL == rows:
            break
        for v in range(len(r)):
            for j in range(n):
                weights[at + 8 * v : at + 8 * v + 8, 128 * j : 128 * j + 128] = r[v][j] * scale[v]
        if at:
            weights[at - TALL : at, :] = jnp.zeros((TALL, 128 * n), F32)
        panel[at + TALL : rows, :] -= mm(panel[at + TALL : rows, 0:128], weights[...])
    return pivots


def masked_rows(values, ocean):
    place = lax.broadcasted_iota(jnp.int32, (values.shape[0], 1), 0)
    return jnp.where(place < ocean, values, jnp.zeros_like(values))


def put_gram(ocean, masked, out_ref):
    row = lax.broadcasted_iota(jnp.int32, (128, 128), 0)
    col = lax.broadcasted_iota(jnp.int32, (128, 128), 1)
    corner = jnp.logical_and(row == 127, col == 0)
    for i in range(4):
        product = lax.dot_general(
            masked[:, 128 * i : 128 * i + 128], masked[:, 128 * i :], TN, preferred_element_type=F32
        )
        for j in range(i, 4):
            block = product[:, 128 * (j - i) : 128 * (j - i) + 128]
            if i == j == 0:
                block = jnp.where(corner, ocean.astype(F32), block)
            out_ref[16 * AT[i, j] : 16 * AT[i, j] + 16] = block.reshape(16, 8, 128)


class Stream:
    SCRATCH = 17

    def __init__(self, spec, start, refs, me, device, partner, own, mine):
        self.a, self.b, self.c, tiles = spec
        self.na, self.nb, self.nc = SIZE[self.a], SIZE[self.b], SIZE[self.c]
        self.unit = tiles // (self.na * self.nb)
        self.start = start
        self.from_a, self.sum_a, self.from_b, self.sum_b, self.from_c = refs[:5]
        self.sems = refs[5:]
        self.me, self.device, self.partner = me, device, partner
        self.own, self.mine = own, mine
        self.started, self.live = [], []

    @staticmethod
    def scratch(spec):
        a, b, c, tiles = spec
        na, nb, nc = SIZE[a], SIZE[b], SIZE[c]
        unit = tiles // (na * nb)
        shapes = [(na - 1, nb * unit), (nb * unit,), (nb - 1, unit), (unit,), (nc, unit)]
        sems = []
        for n in (na - 1, nb - 1, nc - 1, nb - 1, na - 1, na):
            sems += [pltpu.SemaphoreType.DMA((n,))] * 2
        return [pltpu.VMEM((*shape, 8, 128), F32) for shape in shapes] + sems

    def part(self, i):
        return pl.ds(self.start + i * (self.nb * self.unit), self.nb * self.unit)

    def piece(self, i, j):
        return pl.ds(self.start + (i * self.nb + j) * self.unit, self.unit)

    def send(self, phase, k, src, dst, device):
        copy = pltpu.make_async_remote_copy(
            src_ref=src,
            dst_ref=dst,
            send_sem=self.sems[2 * phase].at[k],
            recv_sem=self.sems[2 * phase + 1].at[k],
            device_id=device,
            device_id_type=MESH,
        )
        copy.start()
        self.started.append(copy)
        return copy

    def to_all(self, phase, axis, src, dst):
        size = SIZE[axis]
        self.live = []
        for k, far in enumerate(FAR[size]):
            other = (self.me[axis] + far) % size
            self.live.append(self.send(phase, k, src(other), dst(k), self.device[axis](other)))

    def received(self):
        for copy in self.live:
            copy.wait_recv()

    def scatter_a(self):
        self.to_all(0, self.a, lambda o: self.own.at[self.part(o)], lambda k: self.from_a.at[k])

    def scatter_b(self):
        self.received()
        total = self.own[self.part(self.me[self.a])]
        for k in range(self.na - 1):
            total = total + self.from_a[k]
        self.sum_a[...] = total
        unit = self.unit
        self.to_all(
            1, self.b, lambda o: self.sum_a.at[pl.ds(o * unit, unit)], lambda k: self.from_b.at[k]
        )

    def exchange_c(self):
        self.received()
        total = self.sum_a[pl.ds(self.me[self.b] * self.unit, self.unit)]
        for k in range(self.nb - 1):
            total = total + self.from_b[k]
        self.sum_b[...] = total
        place = self.me[self.c]
        self.to_all(2, self.c, lambda o: self.sum_b, lambda k: self.from_c.at[place])
        self.from_c[place] = total

    def gather_b(self):
        self.received()
        total = self.from_c[0]
        for k in range(1, self.nc):
            total = total + self.from_c[k]
        at = self.piece(self.me[self.a], self.me[self.b])
        self.mine[at] = total
        self.to_all(3, self.b, lambda o: self.mine.at[at], lambda k: self.mine.at[at])

    def gather_a(self):
        self.received()
        at = self.part(self.me[self.a])
        self.to_all(4, self.a, lambda o: self.mine.at[at], lambda k: self.mine.at[at])

    def over(self, k):
        far = (0, *FAR[self.na])[k]
        at = self.part((self.me[self.a] + self.na - far) % self.na)
        return pltpu.make_async_remote_copy(
            src_ref=self.mine.at[at],
            dst_ref=self.mine.at[at],
            send_sem=self.sems[10].at[k],
            recv_sem=self.sems[11].at[k],
            device_id=self.partner,
            device_id_type=MESH,
        )

    def hand_over(self):
        for k in range(self.na):
            if k:
                self.live[k - 1].wait_recv()
            self.over(k).start()

    def taken_over(self, theirs):
        for k in range(self.na):
            far = (0, *FAR[self.na])[k]
            at = self.part((self.me[self.a] + self.na - far) % self.na)
            pltpu.make_async_remote_copy(
                src_ref=theirs.at[at],
                dst_ref=theirs.at[at],
                send_sem=self.sems[10].at[k],
                recv_sem=self.sems[11].at[k],
                device_id=self.partner,
                device_id_type=MESH,
            ).wait_recv()


def times_gram(left, block):
    done = []
    for j in range(4):
        total = None
        for i in range(4):
            piece = left[:, 128 * i : 128 * i + 128]
            term = mm(piece, block(i, j)) if i <= j else mm(piece, block(j, i), NT)
            total = term if total is None else total + term
        done.append(total)
    return jnp.concatenate(done, axis=1)


def square(product):
    return jnp.concatenate([product, jnp.zeros_like(product)], axis=1)


def whole_kernel(
    ocean_ref, st_hbm, values_hbm, masked, fin, line,
    own, both, a, u, w, e, eu, xt, st_ref, loaded, brought, go, sx, rx, sl, rl, *refs
):
    field = lax.axis_index("field")
    y = lax.axis_index("group")
    row = lax.axis_index("row")
    z, x = row // NX, row % NX
    me = {"x": x, "y": y, "z": z}
    device = {
        "x": lambda other: (field, y, z * NX + other),
        "y": lambda other: (field, other, row),
        "z": lambda other: (field, y, other * NX + x),
    }
    partner = (1 - field, y, row)
    first, second = field == 0, field == 1
    barrier = pltpu.get_barrier_semaphore()
    everyone = [partner]
    for axis, size in SIZE.items():
        everyone += [device[axis]((me[axis] + far) % size) for far in FAR[size]]
    for other in everyone:
        pl.semaphore_signal(barrier, inc=1, device_id=other, device_id_type=MESH)
    load = pltpu.make_async_copy(values_hbm, masked, loaded)
    load.start()
    bring = pltpu.make_async_copy(st_hbm, st_ref, brought)
    bring.start()
    load.wait()
    bring.wait()
    masked[...] = masked_rows(masked[...], ocean_ref[0, 0])
    put_gram(ocean_ref[0, 0], masked, own)
    pl.semaphore_wait(barrier, len(everyone))

    streams, start = [], 0
    for k, spec in enumerate(STREAMS):
        mine = refs[Stream.SCRATCH * k : Stream.SCRATCH * (k + 1)]
        streams.append(Stream(spec, start, mine, me, device, partner, own, both.at[field]))
        start += spec[3]

    for stream in streams:
        stream.scatter_a()
    for stream in streams:
        stream.scatter_b()

    for step in ("exchange_c", "gather_b"):
        for stream in streams:
            getattr(stream, step)()

    @pl.when(first)
    def _():
        pl.semaphore_wait(go, 1)

    for stream in streams:
        stream.gather_a()

    line_row = lax.broadcasted_iota(jnp.int32, (128, 128), 0)
    line_col = lax.broadcasted_iota(jnp.int32, (128, 128), 1)
    corner = jnp.logical_and(line_row == 127, line_col == 0)

    def raw(f, at):
        return both[f, 16 * at : 16 * at + 16].reshape(128, 128)

    def scaled(f, at, rate):
        block = raw(f, at)
        if at == 0:
            block = jnp.where(corner, block[0:1, 127:128], block)
        return block * rate

    def rate_of(f):
        return 1.0 / raw(f, 0)[127:128, 0:1]

    def across_chip(j):
        return pltpu.make_async_remote_copy(
            src_ref=xt.at[j], dst_ref=xt.at[j], send_sem=sx.at[j], recv_sem=rx.at[j],
            device_id=partner, device_id_type=MESH,
        )

    def strengths_across():
        return pltpu.make_async_remote_copy(
            src_ref=line, dst_ref=line, send_sem=sl, recv_sem=rl,
            device_id=partner, device_id_type=MESH,
        )

    @pl.when(first)
    def _():
        for stream in streams:
            stream.hand_over()
        for j in range(4):
            across_chip(j).wait_recv()

    @pl.when(second)
    def _():
        for stream in streams:
            stream.received()
        pl.semaphore_signal(go, inc=1, device_id=partner, device_id_type=MESH)
        rate = rate_of(1)
        for i, j in BLOCKS:
            a[128 * i : 128 * i + 128, 128 * j : 128 * j + 128] = scaled(1, AT[i, j], rate)
        for i in range(4):
            lo, n = 128 * i, 512 - 128 * i
            at = pl.ds(lo, 128)
            eliminate(a.at[at, lo:512], u.at[at, lo:512], w.at[:, 0:n], 128)
            for j in range(i + 1, 4):
                turned = u[lo : lo + 128, 128 * j : 128 * j + 128].T
                a[128 * j : 128 * j + 128, 128 * j : 512] -= mm(turned, u[lo : lo + 128, 128 * j : 512])
            total = None
            for k in range(i + 1):
                block = u[128 * k : 128 * k + 128, lo : lo + 128]
                if k == i:
                    block = jnp.where(line_row <= line_col, block, 0.0)
                term = mm(st_ref[:, 128 * k : 128 * k + 128], block)
                total = term if total is None else total + term
            xt[i] = total
            across_chip(i).start()
        for stream in streams:
            stream.taken_over(both.at[0])

    rate0 = rate_of(0)
    left = jnp.concatenate([xt[j] for j in range(4)], axis=1)
    zt = times_gram(left, lambda i, j: scaled(0, AT[i, j], rate0))
    e[:, 128:640] = jnp.where(first, left, zt)
    e[:, 0:128] = square(mm(left, zt, NT))
    eliminate(e, eu, w.at[:, 0:640], 64)

    @pl.when(first)
    def _():
        fin[...] = eu[:, 128:640]

    @pl.when(second)
    def _():
        rate1 = rate_of(1)
        yt = eu[:, 128:640]
        ft = times_gram(yt, lambda i, j: scaled(1, AT[i, j], rate1))
        e[:, 0:128] = square(mm(ft, yt, NT))
        e[:, 128:640] = yt
        pivots = eliminate(e, eu, w.at[:, 0:640], 64)
        fin[...] = eu[:, 128:640]
        lane = lax.broadcasted_iota(jnp.int32, (8, 128), 1)
        drawn = jnp.zeros((8, 128), F32)
        for k, pivot in enumerate(pivots):
            drawn = jnp.where(lane == k, pivot, drawn)
        line[...] = drawn
        strengths_across().start()

    @pl.when(first)
    def _():
        strengths_across().wait_recv()
        for stream in streams:
            for k in range(stream.na):
                stream.over(k).wait_send()

    @pl.when(second)
    def _():
        strengths_across().wait_send()
        for j in range(4):
            across_chip(j).wait_send()

    for stream in streams:
        for copy in stream.started:
            copy.wait_send()


def whole(ocean, st, values):
    scratch = []
    for spec in STREAMS:
        scratch += Stream.scratch(spec)
    vm = pl.BlockSpec(memory_space=pltpu.VMEM)
    return pl.pallas_call(
        whole_kernel,
        out_shape=(
            jax.ShapeDtypeStruct((1024, 512), BF16),
            jax.ShapeDtypeStruct((64, 512), F32),
            jax.ShapeDtypeStruct((8, 128), F32),
        ),
        in_specs=[pl.BlockSpec(memory_space=pltpu.SMEM)] + [pl.BlockSpec(memory_space=pltpu.HBM)] * 2,
        out_specs=(vm, vm, vm),
        scratch_shapes=[
            pltpu.VMEM((160, 8, 128), F32),
            pltpu.VMEM((2, 160, 8, 128), F32),
            pltpu.VMEM((512, 512), F32),
            pltpu.VMEM((512, 512), F32),
            pltpu.VMEM((128, 640), F32),
            pltpu.VMEM((64, 640), F32),
            pltpu.VMEM((64, 640), F32),
            pltpu.VMEM((4, 64, 128), F32),
            pltpu.VMEM((64, 512), F32),
            pltpu.SemaphoreType.DMA,
            pltpu.SemaphoreType.DMA,
            pltpu.SemaphoreType.REGULAR,
            pltpu.SemaphoreType.DMA((4,)),
            pltpu.SemaphoreType.DMA((4,)),
            pltpu.SemaphoreType.DMA,
            pltpu.SemaphoreType.DMA,
        ]
        + scratch,
        compiler_params=pltpu.CompilerParams(
            collective_id=0, has_side_effects=True, vmem_limit_bytes=419 * 2**17
        ),
    )(ocean, st, values)


def patterns_kernel(masked_ref, fin_ref, line_ref, out_ref, strengths_ref):
    wh, wl = split(fin_ref[...])
    halves = lax.dot_general(
        jnp.concatenate([wh, wl], axis=0), masked_ref[...], NT, preferred_element_type=F32
    )
    out_ref[...] = halves[0:64] + halves[64:128]
    strengths_ref[...] = line_ref[0:1, 0:64]


def patterns_of(masked, fin, line):
    vm = pl.BlockSpec(memory_space=pltpu.VMEM)
    return pl.pallas_call(
        patterns_kernel,
        out_shape=(jax.ShapeDtypeStruct((64, 1024), F32), jax.ShapeDtypeStruct((1, 64), F32)),
        in_specs=[vm] * 3,
        out_specs=(vm, vm),
        compiler_params=pltpu.CompilerParams(vmem_limit_bytes=32 * 2**20),
    )(masked, fin, line)


def per_device(anomalies, valid_rows, start_basis):
    kept = whole(valid_rows, start_basis.T, anomalies[0])
    patterns, strengths = patterns_of(*kept)
    return patterns.T[None], strengths.reshape(64)


def solution(mesh):
    shards = ("group", "row")
    in_specs = (P("field", shards, None), P("field", shards), P())
    out_specs = (P("field", shards, None), P())
    return jax.shard_map(
        per_device, mesh=mesh, in_specs=in_specs, out_specs=out_specs, check_vma=False
    )
```

```python
import functools

import jax
import jax.numpy as jnp
from jax import lax
from jax.experimental import pallas as pl
from jax.experimental.pallas import tpu as pltpu
from jax.sharding import PartitionSpec as P

F32, BF16 = jnp.float32, jnp.bfloat16
NN = (((1,), (0,)), ((), ()))
NT = (((1,), (1,)), ((), ()))
TN = (((0,), (0,)), ((), ()))
MESH = pl.DeviceIdType.MESH
NX = 4
SIZE = {"x": NX, "y": 8, "z": 8}
FAR = {4: (1, 3, 2), 8: (1, 7, 2, 6, 3, 5, 4)}
STREAMS = (("x", "y", "z", 64), ("z", "x", "y", 32), ("x", "z", "y", 64))
TALL = 16
BLOCKS = [(i, j) for i in range(4) for j in range(i, 4)]
AT = {pair: at for at, pair in enumerate(BLOCKS)}


def split(x):
    hi = x.astype(BF16)
    return hi, (x - hi.astype(F32)).astype(BF16)


def mm(a, b, dims=NN):
    ah, al = split(a)
    bh, bl = split(b)
    dot = functools.partial(lax.dot_general, dimension_numbers=dims, preferred_element_type=F32)
    return dot(ah, bh) + (dot(ah, bl) + dot(al, bh))


def across(x, k):
    return jnp.broadcast_to(x[k : k + 1, :], (8, 128))


def along(x, k):
    return jnp.broadcast_to(x[:, k : k + 1], (8, 128))


def eliminate(panel, upper, weights, rows):
    n = panel.shape[1] // 128
    sub = lax.broadcasted_iota(jnp.int32, (8, 128), 0)
    weights[...] = jnp.zeros_like(weights)
    pivots = []
    for at in range(0, rows, TALL):
        r = [
            [panel[at + 8 * v : at + 8 * v + 8, 128 * j : 128 * j + 128] for j in range(n)]
            for v in range(TALL // 8)
        ]
        c = [[along(r[v][0], at + k) for k in range(TALL)] for v in range(TALL // 8)]
        scale = [None] * len(r)
        kept = [[None] * n for _ in r]
        for k in range(TALL):
            o, s = divmod(k, 8)
            d = across(c[o][k], s)
            p = 1.0 / d
            root = lax.rsqrt(d)
            pivots.append(d[0:1] * root[0:1])
            scale[o] = p if s == 0 else jnp.where(sub >= s, p, scale[o])
            m = [c[v][k] * p for v in range(len(r))]
            m[o] = jnp.where(sub == s, 0.0, m[o])
            for j in range(n):
                row = across(r[o][j], s)
                now = r[o][j] * root
                kept[o][j] = now if s == 0 else jnp.where(sub >= s, now, kept[o][j])
                for v in range(len(r)):
                    r[v][j] = r[v][j] - m[v] * row
            for q in range(k + 1, TALL):
                row = across(c[o][q], s)
                for v in range(len(r)):
                    c[v][q] = c[v][q] - m[v] * row
        for v in range(len(r)):
            for j in range(n):
                upper[at + 8 * v : at + 8 * v + 8, 128 * j : 128 * j + 128] = kept[v][j]
        if at + TALL == rows:
            break
        for v in range(len(r)):
            for j in range(n):
                weights[at + 8 * v : at + 8 * v + 8, 128 * j : 128 * j + 128] = r[v][j] * scale[v]
        if at:
            weights[at - TALL : at, :] = jnp.zeros((TALL, 128 * n), F32)
        panel[at + TALL : rows, :] -= mm(panel[at + TALL : rows, 0:128], weights[...])
    return pivots


def masked_rows(values, ocean):
    place = lax.broadcasted_iota(jnp.int32, (values.shape[0], 1), 0)
    return jnp.where(place < ocean, values, jnp.zeros_like(values))


def put_gram(ocean, masked, out_ref, block_rows):
    row = lax.broadcasted_iota(jnp.int32, (128, 128), 0)
    col = lax.broadcasted_iota(jnp.int32, (128, 128), 1)
    corner = jnp.logical_and(row == 127, col == 0)
    for i in block_rows:
        product = lax.dot_general(
            masked[:, 128 * i : 128 * i + 128], masked[:, 128 * i :], TN, preferred_element_type=F32
        )
        for j in range(i, 4):
            block = product[:, 128 * (j - i) : 128 * (j - i) + 128]
            if i == j == 0:
                block = jnp.where(corner, ocean.astype(F32), block)
            out_ref[16 * AT[i, j] : 16 * AT[i, j] + 16] = block.reshape(16, 8, 128)


class Stream:
    SCRATCH = 17

    def __init__(self, spec, start, refs, me, device, partner, own, mine):
        self.a, self.b, self.c, tiles = spec
        self.na, self.nb, self.nc = SIZE[self.a], SIZE[self.b], SIZE[self.c]
        self.unit = tiles // (self.na * self.nb)
        self.start = start
        self.from_a, self.sum_a, self.from_b, self.sum_b, self.from_c = refs[:5]
        self.sems = refs[5:]
        self.me, self.device, self.partner = me, device, partner
        self.own, self.mine = own, mine
        self.started, self.live = [], []

    @staticmethod
    def scratch(spec):
        a, b, c, tiles = spec
        na, nb, nc = SIZE[a], SIZE[b], SIZE[c]
        unit = tiles // (na * nb)
        shapes = [(na - 1, nb * unit), (nb * unit,), (nb - 1, unit), (unit,), (nc, unit)]
        sems = []
        for n in (na - 1, nb - 1, nc - 1, nb - 1, na - 1, na):
            sems += [pltpu.SemaphoreType.DMA((n,))] * 2
        return [pltpu.VMEM((*shape, 8, 128), F32) for shape in shapes] + sems

    def part(self, i):
        return pl.ds(self.start + i * (self.nb * self.unit), self.nb * self.unit)

    def piece(self, i, j):
        return pl.ds(self.start + (i * self.nb + j) * self.unit, self.unit)

    def send(self, phase, k, src, dst, device):
        copy = pltpu.make_async_remote_copy(
            src_ref=src,
            dst_ref=dst,
            send_sem=self.sems[2 * phase].at[k],
            recv_sem=self.sems[2 * phase + 1].at[k],
            device_id=device,
            device_id_type=MESH,
        )
        copy.start()
        self.started.append(copy)
        return copy

    def to_all(self, phase, axis, src, dst):
        size = SIZE[axis]
        self.live = []
        for k, far in enumerate(FAR[size]):
            other = (self.me[axis] + far) % size
            self.live.append(self.send(phase, k, src(other), dst(k), self.device[axis](other)))

    def received(self):
        for copy in self.live:
            copy.wait_recv()

    def scatter_a(self):
        self.to_all(0, self.a, lambda o: self.own.at[self.part(o)], lambda k: self.from_a.at[k])

    def scatter_b(self):
        self.received()
        total = self.own[self.part(self.me[self.a])]
        for k in range(self.na - 1):
            total = total + self.from_a[k]
        self.sum_a[...] = total
        unit = self.unit
        self.to_all(
            1, self.b, lambda o: self.sum_a.at[pl.ds(o * unit, unit)], lambda k: self.from_b.at[k]
        )

    def exchange_c(self):
        self.received()
        total = self.sum_a[pl.ds(self.me[self.b] * self.unit, self.unit)]
        for k in range(self.nb - 1):
            total = total + self.from_b[k]
        self.sum_b[...] = total
        place = self.me[self.c]
        self.to_all(2, self.c, lambda o: self.sum_b, lambda k: self.from_c.at[place])
        self.from_c[place] = total

    def gather_b(self):
        self.received()
        total = self.from_c[0]
        for k in range(1, self.nc):
            total = total + self.from_c[k]
        at = self.piece(self.me[self.a], self.me[self.b])
        self.mine[at] = total
        self.to_all(3, self.b, lambda o: self.mine.at[at], lambda k: self.mine.at[at])

    def gather_a(self):
        self.received()
        at = self.part(self.me[self.a])
        self.to_all(4, self.a, lambda o: self.mine.at[at], lambda k: self.mine.at[at])

    def over(self, k):
        far = (0, *FAR[self.na])[k]
        at = self.part((self.me[self.a] + self.na - far) % self.na)
        return pltpu.make_async_remote_copy(
            src_ref=self.mine.at[at],
            dst_ref=self.mine.at[at],
            send_sem=self.sems[10].at[k],
            recv_sem=self.sems[11].at[k],
            device_id=self.partner,
            device_id_type=MESH,
        )

    def hand_over(self):
        for k in range(self.na):
            if k:
                self.live[k - 1].wait_recv()
            self.over(k).start()

    def taken_over(self, theirs):
        for k in range(self.na):
            far = (0, *FAR[self.na])[k]
            at = self.part((self.me[self.a] + self.na - far) % self.na)
            pltpu.make_async_remote_copy(
                src_ref=theirs.at[at],
                dst_ref=theirs.at[at],
                send_sem=self.sems[10].at[k],
                recv_sem=self.sems[11].at[k],
                device_id=self.partner,
                device_id_type=MESH,
            ).wait_recv()


def times_gram(left, block):
    done = []
    for j in range(4):
        total = None
        for i in range(4):
            piece = left[:, 128 * i : 128 * i + 128]
            term = mm(piece, block(i, j)) if i <= j else mm(piece, block(j, i), NT)
            total = term if total is None else total + term
        done.append(total)
    return jnp.concatenate(done, axis=1)


def square(product):
    return jnp.concatenate([product, jnp.zeros_like(product)], axis=1)


def whole_kernel(
    ocean_ref, st_hbm, values_hbm, masked, fin, line,
    own, both, a, u, w, e, eu, xt, st_ref, loaded, brought, go, sx, rx, sl, rl, *refs
):
    field = lax.axis_index("field")
    y = lax.axis_index("group")
    row = lax.axis_index("row")
    z, x = row // NX, row % NX
    me = {"x": x, "y": y, "z": z}
    device = {
        "x": lambda other: (field, y, z * NX + other),
        "y": lambda other: (field, other, row),
        "z": lambda other: (field, y, other * NX + x),
    }
    partner = (1 - field, y, row)
    first, second = field == 0, field == 1
    barrier = pltpu.get_barrier_semaphore()
    everyone = [partner]
    for axis, size in SIZE.items():
        everyone += [device[axis]((me[axis] + far) % size) for far in FAR[size]]
    for other in everyone:
        pl.semaphore_signal(barrier, inc=1, device_id=other, device_id_type=MESH)
    load = pltpu.make_async_copy(values_hbm, masked, loaded)
    load.start()
    bring = pltpu.make_async_copy(st_hbm, st_ref, brought)
    bring.start()
    load.wait()
    bring.wait()
    masked[...] = masked_rows(masked[...], ocean_ref[0, 0])
    put_gram(ocean_ref[0, 0], masked, own, (0,))
    pl.semaphore_wait(barrier, len(everyone))

    streams, start = [], 0
    for k, spec in enumerate(STREAMS):
        mine = refs[Stream.SCRATCH * k : Stream.SCRATCH * (k + 1)]
        streams.append(Stream(spec, start, mine, me, device, partner, own, both.at[field]))
        start += spec[3]

    streams[0].scatter_a()
    put_gram(ocean_ref[0, 0], masked, own, (1, 2, 3))
    for stream in streams[1:]:
        stream.scatter_a()
    for stream in streams:
        stream.scatter_b()

    for step in ("exchange_c", "gather_b"):
        for stream in streams:
            getattr(stream, step)()

    @pl.when(first)
    def _():
        pl.semaphore_wait(go, 1)

    for stream in streams:
        stream.gather_a()

    line_row = lax.broadcasted_iota(jnp.int32, (128, 128), 0)
    line_col = lax.broadcasted_iota(jnp.int32, (128, 128), 1)
    corner = jnp.logical_and(line_row == 127, line_col == 0)

    def raw(f, at):
        return both[f, 16 * at : 16 * at + 16].reshape(128, 128)

    def scaled(f, at, rate):
        block = raw(f, at)
        if at == 0:
            block = jnp.where(corner, block[0:1, 127:128], block)
        return block * rate

    def rate_of(f):
        return 1.0 / raw(f, 0)[127:128, 0:1]

    def across_chip(j):
        return pltpu.make_async_remote_copy(
            src_ref=xt.at[j], dst_ref=xt.at[j], send_sem=sx.at[j], recv_sem=rx.at[j],
            device_id=partner, device_id_type=MESH,
        )

    def strengths_across():
        return pltpu.make_async_remote_copy(
            src_ref=line, dst_ref=line, send_sem=sl, recv_sem=rl,
            device_id=partner, device_id_type=MESH,
        )

    @pl.when(first)
    def _():
        for stream in streams:
            stream.hand_over()
        for j in range(4):
            across_chip(j).wait_recv()

    @pl.when(second)
    def _():
        streams[0].received()
        pl.semaphore_signal(go, inc=1, device_id=partner, device_id_type=MESH)
        rate = rate_of(1)
        for i in range(4):
            if i == 1:
                for stream in streams[1:]:
                    stream.received()
                for k, j in BLOCKS:
                    if k:
                        later = scaled(1, AT[k, j], rate)
                        turned = u[0:128, 128 * k : 128 * k + 128].T
                        later = later - mm(turned, u[0:128, 128 * j : 128 * j + 128])
                        a[128 * k : 128 * k + 128, 128 * j : 128 * j + 128] = later
            elif i == 0:
                for j in range(4):
                    a[0:128, 128 * j : 128 * j + 128] = scaled(1, AT[0, j], rate)
            lo, n = 128 * i, 512 - 128 * i
            at = pl.ds(lo, 128)
            eliminate(a.at[at, lo:512], u.at[at, lo:512], w.at[:, 0:n], 128)
            for j in range(i + 1, 4) if i else ():
                turned = u[lo : lo + 128, 128 * j : 128 * j + 128].T
                a[128 * j : 128 * j + 128, 128 * j : 512] -= mm(turned, u[lo : lo + 128, 128 * j : 512])
            total = None
            for k in range(i + 1):
                block = u[128 * k : 128 * k + 128, lo : lo + 128]
                if k == i:
                    block = jnp.where(line_row <= line_col, block, 0.0)
                term = mm(st_ref[:, 128 * k : 128 * k + 128], block)
                total = term if total is None else total + term
            xt[i] = total
            across_chip(i).start()
        for stream in streams:
            stream.taken_over(both.at[0])

    rate0 = rate_of(0)
    left = jnp.concatenate([xt[j] for j in range(4)], axis=1)
    zt = times_gram(left, lambda i, j: scaled(0, AT[i, j], rate0))
    e[:, 128:640] = jnp.where(first, left, zt)
    e[:, 0:128] = square(mm(left, zt, NT))
    eliminate(e, eu, w.at[:, 0:640], 64)

    @pl.when(first)
    def _():
        fin[...] = eu[:, 128:640]

    @pl.when(second)
    def _():
        rate1 = rate_of(1)
        yt = eu[:, 128:640]
        ft = times_gram(yt, lambda i, j: scaled(1, AT[i, j], rate1))
        e[:, 0:128] = square(mm(ft, yt, NT))
        e[:, 128:640] = yt
        pivots = eliminate(e, eu, w.at[:, 0:640], 64)
        fin[...] = eu[:, 128:640]
        lane = lax.broadcasted_iota(jnp.int32, (8, 128), 1)
        drawn = jnp.zeros((8, 128), F32)
        for k, pivot in enumerate(pivots):
            drawn = jnp.where(lane == k, pivot, drawn)
        line[...] = drawn
        strengths_across().start()

    @pl.when(first)
    def _():
        strengths_across().wait_recv()
        for stream in streams:
            for k in range(stream.na):
                stream.over(k).wait_send()

    @pl.when(second)
    def _():
        strengths_across().wait_send()
        for j in range(4):
            across_chip(j).wait_send()

    for stream in streams:
        for copy in stream.started:
            copy.wait_send()


def whole(ocean, st, values):
    scratch = []
    for spec in STREAMS:
        scratch += Stream.scratch(spec)
    vm = pl.BlockSpec(memory_space=pltpu.VMEM)
    return pl.pallas_call(
        whole_kernel,
        out_shape=(
            jax.ShapeDtypeStruct((1024, 512), BF16),
            jax.ShapeDtypeStruct((64, 512), F32),
            jax.ShapeDtypeStruct((8, 128), F32),
        ),
        in_specs=[pl.BlockSpec(memory_space=pltpu.SMEM)] + [pl.BlockSpec(memory_space=pltpu.HBM)] * 2,
        out_specs=(vm, vm, vm),
        scratch_shapes=[
            pltpu.VMEM((160, 8, 128), F32),
            pltpu.VMEM((2, 160, 8, 128), F32),
            pltpu.VMEM((512, 512), F32),
            pltpu.VMEM((512, 512), F32),
            pltpu.VMEM((128, 640), F32),
            pltpu.VMEM((64, 640), F32),
            pltpu.VMEM((64, 640), F32),
            pltpu.VMEM((4, 64, 128), F32),
            pltpu.VMEM((64, 512), F32),
            pltpu.SemaphoreType.DMA,
            pltpu.SemaphoreType.DMA,
            pltpu.SemaphoreType.REGULAR,
            pltpu.SemaphoreType.DMA((4,)),
            pltpu.SemaphoreType.DMA((4,)),
            pltpu.SemaphoreType.DMA,
            pltpu.SemaphoreType.DMA,
        ]
        + scratch,
        compiler_params=pltpu.CompilerParams(
            collective_id=0, has_side_effects=True, vmem_limit_bytes=419 * 2**17
        ),
    )(ocean, st, values)


def patterns_kernel(masked_ref, fin_ref, line_ref, out_ref, strengths_ref):
    wh, wl = split(fin_ref[...])
    halves = lax.dot_general(
        jnp.concatenate([wh, wl], axis=0), masked_ref[...], NT, preferred_element_type=F32
    )
    out_ref[...] = halves[0:64] + halves[64:128]
    strengths_ref[...] = line_ref[0:1, 0:64]


def patterns_of(masked, fin, line):
    vm = pl.BlockSpec(memory_space=pltpu.VMEM)
    return pl.pallas_call(
        patterns_kernel,
        out_shape=(jax.ShapeDtypeStruct((64, 1024), F32), jax.ShapeDtypeStruct((1, 64), F32)),
        in_specs=[vm] * 3,
        out_specs=(vm, vm),
        compiler_params=pltpu.CompilerParams(vmem_limit_bytes=32 * 2**20),
    )(masked, fin, line)


def per_device(anomalies, valid_rows, start_basis):
    kept = whole(valid_rows, start_basis.T, anomalies[0])
    patterns, strengths = patterns_of(*kept)
    return patterns.T[None], strengths.reshape(64)


def solution(mesh):
    shards = ("group", "row")
    in_specs = (P("field", shards, None), P("field", shards), P())
    out_specs = (P("field", shards, None), P())
    return jax.shard_map(
        per_device, mesh=mesh, in_specs=in_specs, out_specs=out_specs, check_vma=False
    )
```
